512 devices in a mesh: side: 2 (over core), row: 8 (over z), vocab: 32 (over y, x).
Axes of the slice: x: 4, y: 8, z: 8, core: 2. Of those that a mesh axis runs over, the one named last changes fastest.
Arguments:
- hidden: bfloat16 [1536, 4096], P('row'), may hold values from -6 to 6
- head: bfloat16 [4096, 81920], P('row', ('side', 'vocab')), may hold values from -8 to 8
- teacher_logits: bfloat16 [1536, 81920], P('row', ('side', 'vocab')), may hold values from -20 to 400
- lengths: int32 [96], replicated, may hold values from 1 to 16, 864 in all
- slot_rollout: int32 [96], replicated, may hold values from 0 to 95, each once
- token_mask: int32 [1536], P('row'), may hold values 0 or 1
Outputs:
- slot_loss: float32 [96], P('row')
- hidden_grad: bfloat16 [1536, 4096], P('row', ('side', 'vocab'))
The draws below stay inside these ranges and needn't reach their ends.
Inputs may be any that keep to these rules, and one draw needn't show every extreme that they name: `lengths`: the longest rollout has exactly 16 scored positions. `slot_rollout`: each rollout stands in exactly one slot.
All inputs are finite; a program needn't handle non-finite values. No bound on the sum of `token_mask` on one device may be relied on, other than what follows from the above.
Results may differ from the reference program's by a relative error of at most 0.0052.
Values may be sent and summed in bfloat16 or wider, within the bound.
No kernel may reach another device: no remote copies, remote signals or barrier semaphores. Data moves between devices by JAX's collectives and lax.ppermute only.
A program may use at most 64 MiB of HBM per device.

```python
import math
import jax
import jax.numpy as jnp
import numpy as np
from jax import lax

D = 4096
VS_DEV = 1280
WIN = 16
TOK_ROW = 192
ROLLOUTS = 96
TOKENS = 1536
VOCAB = 81920
N_ROW = 8


def rising_scale():
    blocks = VOCAB // VS_DEV
    col_block = (jnp.arange(VOCAB) // VS_DEV).astype(jnp.float32)
    return 1.0 + 0.14 * col_block / max(blocks - 1, 1)


def draw_head(key, part):
    key = jax.random.fold_in(key, 7)
    blocks = VOCAB // VS_DEV
    col_block = jnp.arange(VOCAB) // VS_DEV
    pairing = jax.random.permutation(jax.random.fold_in(key, 1), blocks)
    row_block = jnp.arange(D) // (D // blocks)
    spike = jnp.where(row_block[:, None] == pairing[col_block][None, :], 3.0, 1.0)
    base_scale = 2.9 / math.sqrt(D)
    rising = rising_scale()
    base = jax.random.truncated_normal(jax.random.fold_in(key, 2), -5.0, 5.0, (D, VOCAB), jnp.float32)
    values = base * spike * (base_scale * rising)[None, :]
    return values.astype(jnp.bfloat16)


def draw_hidden(key, part):
    key = jax.random.fold_in(key, 11)
    values = jax.random.truncated_normal(jax.random.fold_in(key, 2), -5.0, 5.0, (TOKENS, D), jnp.float32)
    return values.astype(jnp.bfloat16)


def draw_teacher_logits(key, part):
    key = jax.random.fold_in(key, 23)
    rising = rising_scale()
    base = jax.random.truncated_normal(jax.random.fold_in(key, 2), -5.0, 5.0, (TOKENS, VOCAB), jnp.float32)
    values = base * 2.9 * rising[None, :]
    return values.astype(jnp.bfloat16)


def touch_ends(drawn, key, low, largest):
    longest = drawn.shape.index(max(drawn.shape))
    spots = []
    for shift in (0, 1):
        where = [jax.random.randint(jax.random.fold_in(key, axis), (), 0, length) for axis, length in enumerate(drawn.shape)]
        where[longest] = (where[longest] + shift) % drawn.shape[longest]
        spots.append(tuple(where))
    return drawn.at[spots[0]].set(low).at[spots[1]].set(largest)


def length_profile(number_of, total, bound, skew):
    weights = [(1 << 20) // math.isqrt(grade ** skew) + 1 for grade in range(2, number_of + 1)]
    rest, holding = total - bound - (number_of - 1), [1] * (number_of - 1)
    while rest > 0:
        free = [i for i in range(number_of - 1) if holding[i] < bound]
        mass, budget = sum([weights[i] for i in free]), rest
        for i in free:
            extra = min(bound - holding[i], max(1, budget * weights[i] // mass), rest)
            holding[i] = holding[i] + extra
            rest = rest - extra
    return np.array([bound] + holding)


def ragged(rng, amount, total, limit, skew):
    if amount == 2:
        one = jax.random.randint(rng, (), max(1, total - limit), min(limit, total - 1) + 1)
        return jnp.stack([one, total - one])
    tallies = jnp.asarray(length_profile(amount, total, limit, skew), jnp.int32)
    pairs = (amount - 1) // 2
    donor, sink = tallies[1:1 + 2 * pairs:2], tallies[2:2 + 2 * pairs:2]
    slack = jnp.minimum(donor - 1, limit - sink)
    moved = jax.random.randint(jax.random.fold_in(rng, 1), (pairs,), 0, 1 << 20) % (slack + 1)
    tallies = tallies.at[1:1 + 2 * pairs:2].set(donor - moved).at[2:2 + 2 * pairs:2].set(sink + moved)
    return tallies[jax.random.permutation(jax.random.fold_in(rng, 2), amount)]


def setup_inputs(seed: int = 0) -> dict:
    arg_keys = jax.random.split(jax.random.key(seed), 7)
    hidden = draw_hidden(jax.random.fold_in(arg_keys[6], 71), 0)
    head = draw_head(jax.random.fold_in(arg_keys[6], 71), 0)
    teacher_logits = draw_teacher_logits(jax.random.fold_in(arg_keys[6], 71), 0)
    lengths = ragged(arg_keys[3], ROLLOUTS, 9 * ROLLOUTS, WIN, 1).astype(jnp.int32)
    slot_rollout = jax.random.permutation(arg_keys[4], ROLLOUTS).astype(jnp.int32)
    token_mask = touch_ends((jax.random.randint(arg_keys[5], (TOKENS,), 0, 4) < 3).astype(jnp.int32), jax.random.fold_in(arg_keys[5], 1), 0, 1)
    return {"hidden": hidden, "head": head, "teacher_logits": teacher_logits, "lengths": lengths, "slot_rollout": slot_rollout, "token_mask": token_mask}


loss_scale = 256.0


def token_weights(lengths, slot_rollout, token_mask):
    chosen = slot_rollout[:, None] == jnp.arange(ROLLOUTS, dtype=jnp.int32)[None, :]
    slot_length = jnp.sum(jnp.where(chosen, lengths[None, :], 0), axis=1).astype(jnp.int32)
    length_tok = jnp.repeat(slot_length, WIN)
    position = jnp.arange(TOKENS, dtype=jnp.int32) % WIN
    usable = (token_mask > 0) & (position < length_tok)
    return jnp.where(usable, 1.0 / length_tok.astype(jnp.float32), 0.0).astype(jnp.float32)


def reference(hidden, head, teacher_logits, lengths, slot_rollout, token_mask):
    weight = token_weights(lengths, slot_rollout, token_mask)
    hidden_blocks = hidden.reshape(N_ROW, TOK_ROW, D)
    teacher_blocks = teacher_logits.reshape(N_ROW, TOK_ROW, VOCAB)
    weight_blocks = weight.reshape(N_ROW, TOK_ROW)

    def one_block(inputs):
        hidden_rows, teacher_rows, weight_rows = inputs
        logits = jnp.dot(hidden_rows, head, preferred_element_type=jnp.float32)
        student = logits - jax.nn.logsumexp(logits, axis=1, keepdims=True)
        teacher = teacher_rows.astype(jnp.float32)
        teacher_logp = teacher - jax.nn.logsumexp(teacher, axis=1, keepdims=True)
        student_prob = jnp.exp(student)
        diverge = jnp.sum(student_prob * (student - teacher_logp), axis=1)
        logit_grad = (loss_scale * weight_rows[:, None] * student_prob
                      * (student - teacher_logp - diverge[:, None])).astype(jnp.bfloat16)
        hidden_back = lax.dot_general(logit_grad, head, (((1,), (1,)), ((), ())),
                                      preferred_element_type=jnp.float32)
        return diverge, hidden_back.astype(jnp.bfloat16)

    diverge, hidden_back = lax.map(one_block, (hidden_blocks, teacher_blocks, weight_blocks))
    slot_loss = jnp.sum((weight * diverge.reshape(TOKENS)).reshape(ROLLOUTS, WIN), axis=1)
    return slot_loss, hidden_back.reshape(TOKENS, D)
```

```python
import jax
import jax.numpy as jnp
from jax import lax
from jax.sharding import PartitionSpec as P

WIN = 16


loss_scale = 256.0


def swap_side(value):
    return lax.ppermute(value, "side", [(0, 1), (1, 0)])


def from_all(value, count):
    return lax.all_to_all(jnp.broadcast_to(value, (count,) + value.shape), "vocab", 0, 0)


def join(peak, total, term):
    top = jnp.max(peak, axis=0)
    shift = peak - top
    scale = jnp.exp(shift)
    total_all = jnp.sum(total * scale, axis=0)
    if term is None:
        return top, total_all
    return top, total_all, jnp.sum(scale * (term + total * shift), axis=0)


def global_stats(peak, total, term, count):
    rows = [peak, total] if term is None else [peak, total, term]
    own = jnp.stack(rows)
    pair = jnp.stack([own, swap_side(own)])
    own = jnp.stack(join(*[pair[:, i] for i in range(len(rows))], *([None] if term is None else [])))
    gathered = from_all(own, count)
    return join(*[gathered[:, i] for i in range(len(rows))], *([None] if term is None else []))


def body(hidden, head, teacher_logits, lengths, slot_rollout, token_mask):
    tok_rows = hidden.shape[0]
    width = hidden.shape[1]
    count = lax.axis_size("vocab")
    slot_count = tok_rows // WIN
    row_place = lax.axis_index("row")
    side_place = lax.axis_index("side")
    own_slots = lax.dynamic_slice_in_dim(slot_rollout, row_place * slot_count, slot_count)
    chosen = own_slots[:, None] == jnp.arange(lengths.shape[0], dtype=jnp.int32)[None, :]
    slot_length = jnp.sum(jnp.where(chosen, lengths[None, :], 0), axis=1)
    length_tok = jnp.repeat(slot_length, WIN)
    position = jnp.arange(tok_rows, dtype=jnp.int32) % WIN
    usable = (token_mask > 0) & (position < length_tok)
    weight = jnp.where(usable, 1.0 / length_tok.astype(jnp.float32), 0.0)

    columns = lax.all_gather(head, "row", axis=0, tiled=True)

    teacher = teacher_logits.astype(jnp.float32)
    teacher_peak = jnp.max(teacher, axis=1)
    teacher_total = jnp.sum(jnp.exp(teacher - teacher_peak[:, None]), axis=1)
    teacher_peak, teacher_total = global_stats(teacher_peak, teacher_total, None, count)
    teacher_lse = teacher_peak + jnp.log(teacher_total)

    logits = jnp.dot(hidden, columns, preferred_element_type=jnp.float32)
    local_peak = jnp.max(logits, axis=1)
    gap = (logits - local_peak[:, None]) - (teacher - teacher_lse[:, None])
    local_exp = jnp.exp(logits - local_peak[:, None])
    local_total = jnp.sum(local_exp, axis=1)
    local_term = jnp.sum(local_exp * gap, axis=1)
    peak, total, term = global_stats(local_peak, local_total, local_term, count)
    log_total = jnp.log(total)
    diverge = term / total - log_total
    scale = loss_scale * weight / total
    shift = teacher_lse - peak - term / total
    logit_grad = (
        scale[:, None]
        * jnp.exp(logits - peak[:, None])
        * (logits - teacher + shift[:, None])
    ).astype(jnp.bfloat16)
    partial_grad = lax.dot_general(
        logit_grad, columns, (((1,), (1,)), ((), ())), preferred_element_type=jnp.float32
    )
    half = width // 2
    mine = lax.dynamic_slice_in_dim(partial_grad, side_place * half, half, axis=1)
    other = lax.dynamic_slice_in_dim(partial_grad, (1 - side_place) * half, half, axis=1)
    both = mine + swap_side(other)
    lanes = half // count
    packed = both.reshape(2, tok_rows // 2, count, lanes).transpose(2, 1, 0, 3)
    packed = packed.reshape(count, tok_rows // 2, 2 * lanes).astype(jnp.bfloat16)
    pieces = lax.all_to_all(packed, "vocab", 0, 0)
    summed = jnp.sum(pieces.astype(jnp.float32), axis=0).astype(jnp.bfloat16)
    hidden_grad = summed.reshape(tok_rows // 2, 2, lanes).transpose(1, 0, 2).reshape(tok_rows, lanes)
    slot_loss = jnp.sum((weight * diverge).reshape(slot_count, WIN), axis=1)
    return (slot_loss, hidden_grad)


def solution(mesh):
    in_specs = (
        P("row", None),
        P("row", ("side", "vocab")),
        P("row", ("side", "vocab")),
        P(),
        P(),
        P("row"),
    )
    out_specs = (P("row"), P("row", ("side", "vocab")))
    return jax.shard_map(body, mesh=mesh, in_specs=in_specs, out_specs=out_specs, check_vma=False)
```

```python
import functools

import jax
import jax.numpy as jnp
from jax import lax
from jax.experimental import pallas as pl
from jax.experimental.pallas import tpu as pltpu
from jax.sharding import PartitionSpec as P

WIN = 16
HALVES = 2


loss_scale = 256.0


def swap_side(value):
    return lax.ppermute(value, "side", [(0, 1), (1, 0)])


def from_all(value, count):
    return lax.all_to_all(jnp.broadcast_to(value, (count,) + value.shape), "vocab", 0, 0)


def join(peak, total, term):
    top = jnp.max(peak, axis=0)
    shift = peak - top
    scale = jnp.exp(shift)
    total_all = jnp.sum(total * scale, axis=0)
    return top, total_all, jnp.sum(scale * (term + total * shift), axis=0)


def join_pair(own):
    other = swap_side(own)
    return join(*[jnp.stack([own[i], other[i]]) for i in range(own.shape[0])])


def join_vocab(own, count):
    gathered = from_all(own, count)
    return join(*[gathered[:, i] for i in range(own.shape[0])])


def grad_kernel(blocks, place_ref, rows_ref, own_ref, *refs):
    chunk_refs = refs[:-4]
    keep_x, keep_y, send_x, send_y = refs[-4:]
    side = place_ref[0]
    row = place_ref[1]
    step = 1 - 2 * side
    toks = rows_ref.shape[0] // 2
    half_toks = toks // 2
    depth = own_ref.shape[0] // HALVES
    low = lax.broadcasted_iota(jnp.int32, (half_toks, 128), 1) < 64

    def one(chunk, distance, part):
        owner = lax.rem(row - distance * step + blocks, blocks)
        product = lax.dot_general(
            rows_ref[...], chunk, (((1,), (1,)), ((), ())), preferred_element_type=jnp.float32
        )
        pieces = []
        for kind in range(2):
            found = []
            for pair in range(depth // 128):
                lanes = slice(128 * pair, 128 * pair + 128)
                upper = product[kind * toks : kind * toks + half_toks, lanes]
                lower = product[kind * toks + half_toks : (kind + 1) * toks, lanes]
                found.append(jnp.where(low, upper, pltpu.roll(lower, 64, 1)))
                found.append(jnp.where(low, pltpu.roll(upper, 64, 1), lower))
            pieces.append(found)
        first = lax.rem(owner, blocks // 2) * (HALVES * depth // 64) + part * (depth // 64)
        mine = lax.div(owner, blocks // 2) == side

        @pl.when(mine)
        def _():
            for i in range(depth // 64):
                keep_x[first + i] = pieces[0][i]
                keep_y[first + i] = pieces[1][i]

        @pl.when(jnp.logical_not(mine))
        def _():
            for i in range(depth // 64):
                send_x[first + i] = pieces[0][i].astype(send_x.dtype)
                send_y[first + i] = pieces[1][i].astype(send_y.dtype)

    for part in range(HALVES):
        one(own_ref[part * depth : (part + 1) * depth, :], 0, part)
    for index, ref in enumerate(chunk_refs):
        one(ref[...], 1 + index // HALVES, index % HALVES)


def grad_products(place, rows, own, chunks, blocks, count):
    toks, cols = rows.shape[0] // 2, rows.shape[1]
    width = own.shape[0] * blocks
    vmem = pl.BlockSpec(memory_space=pltpu.VMEM)
    shape = (count, toks // 2, 128)
    return pl.pallas_call(
        functools.partial(grad_kernel, blocks),
        out_shape=[jax.ShapeDtypeStruct(shape, jnp.float32)] * 2 + [jax.ShapeDtypeStruct(shape, jnp.bfloat16)] * 2,
        in_specs=[pl.BlockSpec(memory_space=pltpu.SMEM)] + [vmem] * (2 + len(chunks)),
        out_specs=[vmem] * 4,
        compiler_params=pltpu.CompilerParams(vmem_limit_bytes=40 * 1024 * 1024),
        cost_estimate=pl.CostEstimate(
            flops=4 * toks * cols * width, bytes_accessed=2 * cols * width, transcendentals=0
        ),
    )(place, rows, own, *chunks)


def spread(value, lanes):
    split = value.reshape(2, -1)
    return jnp.concatenate([jnp.broadcast_to(split[i][:, None], (split.shape[1], lanes)) for i in range(2)], axis=1)


def body(hidden, head, teacher_logits, lengths, slot_rollout, token_mask):
    tok_rows = hidden.shape[0]
    count = lax.axis_size("vocab")
    blocks = lax.axis_size("row")
    slot_count = tok_rows // WIN
    row_place = lax.axis_index("row")
    side_place = lax.axis_index("side")
    own_slots = lax.dynamic_slice_in_dim(slot_rollout, row_place * slot_count, slot_count)
    chosen = own_slots[:, None] == jnp.arange(lengths.shape[0], dtype=jnp.int32)[None, :]
    slot_length = jnp.sum(jnp.where(chosen, lengths[None, :], 0), axis=1)
    length_tok = jnp.repeat(slot_length, WIN)
    position = jnp.arange(tok_rows, dtype=jnp.int32) % WIN
    usable = (token_mask > 0) & (position < length_tok)
    weight = jnp.where(usable, 1.0 / length_tok.astype(jnp.float32), 0.0)

    full = head.shape[0]
    depth = full // HALVES
    ring = [(i, (i + 1) % blocks) for i in range(blocks)]
    ring += [(blocks + i, blocks + (i - 1) % blocks) for i in range(blocks)]
    step = 1 - 2 * side_place
    held = [head[part * depth : (part + 1) * depth] for part in range(HALVES)]
    logits = jnp.dot(
        lax.dynamic_slice_in_dim(hidden, row_place * full, full, axis=1), head, preferred_element_type=jnp.float32
    )
    chunks = []
    for distance in range(1, blocks):
        held = [lax.ppermute(part, ("side", "row"), ring) for part in held]
        owner = (row_place - distance * step + blocks) % blocks
        for part in range(HALVES):
            piece = lax.dynamic_slice_in_dim(hidden, owner * full + part * depth, depth, axis=1)
            logits = logits + jnp.dot(piece, held[part], preferred_element_type=jnp.float32)
        chunks += held

    teacher = teacher_logits.astype(jnp.float32)
    teacher_peak = jnp.max(teacher, axis=1)
    teacher_total = jnp.sum(jnp.exp(teacher - teacher_peak[:, None]), axis=1)
    teacher_own = jnp.stack([teacher_peak, teacher_total, jnp.zeros_like(teacher_peak)])
    teacher_peak, teacher_total, _ = join_vocab(jnp.stack(join_pair(teacher_own)), count)
    teacher_lse = teacher_peak + jnp.log(teacher_total)

    local_peak = jnp.max(logits, axis=1)
    shifted = logits - local_peak[:, None]
    local_exp = jnp.exp(shifted)
    local_total = jnp.sum(local_exp, axis=1)
    local_term = jnp.sum(local_exp * (shifted - (teacher - teacher_lse[:, None])), axis=1)
    pair_peak, pair_total, pair_term = join_pair(jnp.stack([local_peak, local_total, local_term]))
    pair_mean = pair_term / pair_total
    shifted = logits - pair_peak[:, None]
    pair_exp = jnp.exp(shifted)
    centred = pair_exp * (shifted - (teacher - teacher_lse[:, None]) - pair_mean[:, None])
    rows = jnp.concatenate([centred, pair_exp]).astype(jnp.bfloat16)

    peak, total, term = join_vocab(jnp.stack([pair_peak, pair_total, pair_term]), count)
    mean = term / total
    diverge = mean - jnp.log(total)
    fall = pair_peak - peak
    scale = loss_scale * weight / total * jnp.exp(fall)
    offset = fall + pair_mean - mean

    place = jnp.stack([side_place, row_place]).astype(jnp.int32)
    keep_x, keep_y, send_x, send_y = grad_products(place, rows, head, chunks, blocks, count)
    sum_x = keep_x + swap_side(send_x).astype(jnp.float32)
    sum_y = keep_y + swap_side(send_y).astype(jnp.float32)
    packed = (spread(scale, 64) * (sum_x + spread(offset, 64) * sum_y)).astype(jnp.bfloat16)
    pieces = lax.all_to_all(packed, "vocab", 0, 0)
    summed = jnp.sum(pieces.astype(jnp.float32), axis=0).astype(jnp.bfloat16)
    hidden_grad = jnp.concatenate([summed[:, :64], summed[:, 64:]], axis=0)
    slot_loss = jnp.sum((weight * diverge).reshape(slot_count, WIN), axis=1)
    return (slot_loss, hidden_grad)


def solution(mesh):
    in_specs = (
        P("row", None),
        P("row", ("side", "vocab")),
        P("row", ("side", "vocab")),
        P(),
        P(),
        P("row"),
    )
    out_specs = (P("row"), P("row", ("side", "vocab")))
    return jax.shard_map(body, mesh=mesh, in_specs=in_specs, out_specs=out_specs, check_vma=False)
```

```python
import functools

import jax
import jax.numpy as jnp
from jax import lax
from jax.experimental import pallas as pl
from jax.experimental.pallas import tpu as pltpu
from jax.sharding import PartitionSpec as P

WIN = 16
HALVES = 2
LANES = 128


loss_scale = 256.0


def swap_side(value):
    return lax.ppermute(value, "side", [(0, 1), (1, 0)])


def join(peak, total, teacher_peak, teacher_total, term):
    top = jnp.max(peak, axis=0, keepdims=True)
    teacher_top = jnp.max(teacher_peak, axis=0, keepdims=True)
    shift = peak - top
    teacher_shift = teacher_peak - teacher_top
    scale = jnp.exp(shift)
    return (
        top,
        jnp.sum(total * scale, axis=0, keepdims=True),
        teacher_top,
        jnp.sum(teacher_total * jnp.exp(teacher_shift), axis=0, keepdims=True),
        jnp.sum(scale * (term + total * (shift - teacher_shift)), axis=0, keepdims=True),
    )


def grad_kernel(blocks, place_ref, stats_ref, weight_ref, logits_ref, teacher_ref, own_ref, *refs):
    chunk_refs = refs[:-4]
    keep_ref, send_ref, diverge_ref, grad_ref = refs[-4:]
    side = place_ref[0]
    row = place_ref[1]
    step = 1 - 2 * side
    toks = logits_ref.shape[0]
    rest = toks - LANES
    depth = own_ref.shape[0] // HALVES

    peak, total, teacher_peak, teacher_total, term = join(*[stats_ref[:, i, :] for i in range(5)])
    mean = term / total
    diverge_ref[...] = mean - jnp.log(total) + jnp.log(teacher_total)
    scale = loss_scale * weight_ref[...] / total
    offset = teacher_peak - mean
    table = jnp.concatenate([peak, scale, offset, jnp.zeros((LANES - 3, toks), jnp.float32)], axis=0)
    table = jnp.concatenate([table, jnp.zeros((LANES, 2 * LANES - toks), jnp.float32)], axis=1)
    columns = jnp.transpose(table)[:toks]
    shifted = logits_ref[...] - columns[:, 0:1]
    slope = shifted - teacher_ref[...].astype(jnp.float32) + columns[:, 2:3]
    grad = columns[:, 1:2] * jnp.exp(shifted) * slope
    grad_ref[...] = jnp.transpose(grad).astype(jnp.bfloat16)
    low = lax.broadcasted_iota(jnp.int32, (32, LANES), 1) < rest

    def one(chunk, distance, part):
        owner = lax.rem(row - distance * step + blocks, blocks)
        product = jnp.dot(chunk, grad_ref[...], preferred_element_type=jnp.float32)
        first = lax.rem(owner, blocks // 2) * (HALVES * depth // 64) + part * (depth // 64)
        mine = lax.div(owner, blocks // 2) == side
        wide = jnp.concatenate([product[:, LANES:], jnp.zeros((depth, LANES - rest), jnp.float32)], axis=1)
        pieces = []
        for i in range(depth // 64):
            left = wide[64 * i : 64 * i + 32]
            right = wide[64 * i + 32 : 64 * i + 64]
            pieces.append((product[64 * i : 64 * i + 64, :LANES], jnp.where(low, left, pltpu.roll(right, rest, 1))))

        @pl.when(mine)
        def _():
            for i, (upper, lower) in enumerate(pieces):
                keep_ref[first + i, :64] = upper
                keep_ref[first + i, 64:] = lower

        @pl.when(jnp.logical_not(mine))
        def _():
            for i, (upper, lower) in enumerate(pieces):
                send_ref[first + i, :64] = upper.astype(send_ref.dtype)
                send_ref[first + i, 64:] = lower.astype(send_ref.dtype)

    for part in range(HALVES):
        one(own_ref[part * depth : (part + 1) * depth, :], 0, part)
    for index, ref in enumerate(chunk_refs):
        one(ref[...], 1 + index // HALVES, index % HALVES)


def grad_products(place, stats, weight, logits, teacher, own, chunks, blocks, count):
    toks, cols = logits.shape
    width = own.shape[0] * blocks
    vmem = pl.BlockSpec(memory_space=pltpu.VMEM)
    shape = (count, toks // 2, LANES)
    return pl.pallas_call(
        functools.partial(grad_kernel, blocks),
        out_shape=[
            jax.ShapeDtypeStruct(shape, jnp.float32),
            jax.ShapeDtypeStruct(shape, jnp.bfloat16),
            jax.ShapeDtypeStruct((1, toks), jnp.float32),
        ],
        in_specs=[pl.BlockSpec(memory_space=pltpu.SMEM)] + [vmem] * (5 + len(chunks)),
        out_specs=[vmem] * 3,
        scratch_shapes=[pltpu.VMEM((cols, toks), jnp.bfloat16)],
        compiler_params=pltpu.CompilerParams(vmem_limit_bytes=24 * 1024 * 1024),
        cost_estimate=pl.CostEstimate(
            flops=2 * toks * cols * width, bytes_accessed=2 * cols * width, transcendentals=toks * cols
        ),
    )(place, stats, weight, logits, teacher, own, *chunks)


def body(hidden, head, teacher_logits, lengths, slot_rollout, token_mask):
    tok_rows = hidden.shape[0]
    count = lax.axis_size("vocab")
    blocks = lax.axis_size("row")
    slot_count = tok_rows // WIN
    row_place = lax.axis_index("row")
    side_place = lax.axis_index("side")
    own_slots = lax.dynamic_slice_in_dim(slot_rollout, row_place * slot_count, slot_count)
    chosen = own_slots[:, None] == jnp.arange(lengths.shape[0], dtype=jnp.int32)[None, :]
    slot_length = jnp.sum(jnp.where(chosen, lengths[None, :], 0), axis=1)
    length_tok = jnp.repeat(slot_length, WIN)
    position = jnp.arange(tok_rows, dtype=jnp.int32) % WIN
    usable = (token_mask > 0) & (position < length_tok)
    weight = jnp.where(usable, 1.0 / length_tok.astype(jnp.float32), 0.0)

    full = head.shape[0]
    depth = full // HALVES
    ring = [(i, (i + 1) % blocks) for i in range(blocks)]
    ring += [(blocks + i, blocks + (i - 1) % blocks) for i in range(blocks)]
    step = 1 - 2 * side_place
    held = [head[part * depth : (part + 1) * depth] for part in range(HALVES)]
    logits = jnp.dot(
        lax.dynamic_slice_in_dim(hidden, row_place * full, full, axis=1), head, preferred_element_type=jnp.float32
    )
    chunks = []
    for distance in range(1, blocks):
        held = [lax.ppermute(part, ("side", "row"), ring) for part in held]
        owner = (row_place - distance * step + blocks) % blocks
        for part in range(HALVES):
            piece = lax.dynamic_slice_in_dim(hidden, owner * full + part * depth, depth, axis=1)
            logits = logits + jnp.dot(piece, held[part], preferred_element_type=jnp.float32)
        chunks += held

    teacher = teacher_logits.astype(jnp.float32)
    teacher_peak = jnp.max(teacher, axis=1)
    teacher_gap = teacher - teacher_peak[:, None]
    teacher_total = jnp.sum(jnp.exp(teacher_gap), axis=1)
    peak = jnp.max(logits, axis=1)
    shifted = logits - peak[:, None]
    powers = jnp.exp(shifted)
    total = jnp.sum(powers, axis=1)
    term = jnp.sum(powers * (shifted - teacher_gap), axis=1)
    blank = jnp.zeros_like(peak)
    own = jnp.stack([peak, total, teacher_peak, teacher_total, term, blank, blank, blank])
    other = swap_side(own)
    pair = jnp.concatenate([*join(*[jnp.stack([own[i], other[i]]) for i in range(5)]), own[5:]])
    stats = lax.all_to_all(jnp.broadcast_to(pair, (count,) + pair.shape), "vocab", 0, 0)

    place = jnp.stack([side_place, row_place]).astype(jnp.int32)
    keep, send, diverge = grad_products(
        place, stats, weight[None], logits, teacher_logits, head, chunks, blocks, count
    )
    packed = (keep + swap_side(send).astype(jnp.float32)).astype(jnp.bfloat16)
    pieces = lax.all_to_all(packed, "vocab", 0, 0)
    summed = jnp.sum(pieces.astype(jnp.float32), axis=0).astype(jnp.bfloat16)
    rest = tok_rows - LANES
    lower = jnp.concatenate([summed[64:, :rest], summed[64:, rest:]], axis=0)
    hidden_grad = jnp.concatenate([summed[:64], lower], axis=1).T
    slot_loss = jnp.sum((weight * diverge[0]).reshape(slot_count, WIN), axis=1)
    return (slot_loss, hidden_grad)


def solution(mesh):
    in_specs = (
        P("row", None),
        P("row", ("side", "vocab")),
        P("row", ("side", "vocab")),
        P(),
        P(),
        P("row"),
    )
    out_specs = (P("row"), P("row", ("side", "vocab")))
    return jax.shard_map(body, mesh=mesh, in_specs=in_specs, out_specs=out_specs, check_vma=False)
```

```python
import functools

import jax
import jax.numpy as jnp
from jax import lax
from jax.experimental import pallas as pl
from jax.experimental.pallas import tpu as pltpu
from jax.sharding import PartitionSpec as P

WIN = 16
HALVES = 2
LANES = 128


loss_scale = 256.0


def swap_side(value):
    return lax.ppermute(value, "side", [(0, 1), (1, 0)])


def join(peak, total, teacher_peak, teacher_total, term):
    top = jnp.max(peak, axis=0, keepdims=True)
    teacher_top = jnp.max(teacher_peak, axis=0, keepdims=True)
    shift = peak - top
    teacher_shift = teacher_peak - teacher_top
    scale = jnp.exp(shift)
    return (
        top,
        jnp.sum(total * scale, axis=0, keepdims=True),
        teacher_top,
        jnp.sum(teacher_total * jnp.exp(teacher_shift), axis=0, keepdims=True),
        jnp.sum(scale * (term + total * (shift - teacher_shift)), axis=0, keepdims=True),
    )


def grad_kernel(blocks, place_ref, stats_ref, weight_ref, logits_ref, teacher_ref, own_ref, *refs):
    chunk_refs = refs[:-8]
    keep_ref, send_ref, diverge_ref, grad_ref, logits_buf, teacher_buf, head_buf, sems = refs[-8:]
    side = place_ref[0]
    row = place_ref[1]
    step = 1 - 2 * side
    toks = logits_ref.shape[0]
    rest = toks - LANES
    depth = own_ref.shape[0] // HALVES
    copies = [
        pltpu.make_async_copy(logits_ref, logits_buf, sems.at[0]),
        pltpu.make_async_copy(teacher_ref, teacher_buf, sems.at[1]),
    ]
    sources = [own_ref.at[part * depth : (part + 1) * depth] for part in range(HALVES)] + list(chunk_refs)
    for index, source in enumerate(sources):
        copies.append(pltpu.make_async_copy(source, head_buf.at[index], sems.at[2 + index]))
    for copy in copies:
        copy.start()

    peak, total, teacher_peak, teacher_total, term = join(*[stats_ref[:, i, :] for i in range(5)])
    mean = term / total
    diverge_ref[...] = mean - jnp.log(total) + jnp.log(teacher_total)
    scale = loss_scale * weight_ref[...] / total
    offset = teacher_peak - mean
    table = jnp.concatenate([peak, scale, offset, jnp.zeros((LANES - 3, toks), jnp.float32)], axis=0)
    table = jnp.concatenate([table, jnp.zeros((LANES, 2 * LANES - toks), jnp.float32)], axis=1)
    columns = jnp.transpose(table)[:toks]
    copies[0].wait()
    copies[1].wait()
    shifted = logits_buf[...] - columns[:, 0:1]
    slope = shifted - teacher_buf[...].astype(jnp.float32) + columns[:, 2:3]
    grad = columns[:, 1:2] * jnp.exp(shifted) * slope
    grad_ref[...] = jnp.transpose(grad).astype(jnp.bfloat16)
    low = lax.broadcasted_iota(jnp.int32, (32, LANES), 1) < rest

    def one(product, distance, part):
        owner = lax.rem(row - distance * step + blocks, blocks)
        first = lax.rem(owner, blocks // 2) * (HALVES * depth // 64) + part * (depth // 64)
        mine = lax.div(owner, blocks // 2) == side
        wide = jnp.concatenate([product[:, LANES:], jnp.zeros((depth, LANES - rest), jnp.float32)], axis=1)
        pieces = []
        for i in range(depth // 64):
            left = wide[64 * i : 64 * i + 32]
            right = wide[64 * i + 32 : 64 * i + 64]
            pieces.append((product[64 * i : 64 * i + 64, :LANES], jnp.where(low, left, pltpu.roll(right, rest, 1))))

        @pl.when(mine)
        def _():
            for i, (upper, lower) in enumerate(pieces):
                keep_ref[first + i, :64] = upper
                keep_ref[first + i, 64:] = lower

        @pl.when(jnp.logical_not(mine))
        def _():
            for i, (upper, lower) in enumerate(pieces):
                send_ref[first + i, :64] = upper.astype(send_ref.dtype)
                send_ref[first + i, 64:] = lower.astype(send_ref.dtype)

    for base in range(0, len(sources), HALVES):
        for index in range(base, base + HALVES):
            copies[2 + index].wait()
        block = head_buf[base : base + HALVES].reshape(HALVES * depth, head_buf.shape[2])
        product = jnp.dot(block, grad_ref[...], preferred_element_type=jnp.float32)
        for part in range(HALVES):
            one(product[part * depth : (part + 1) * depth], base // HALVES, part)


def grad_products(place, stats, weight, logits, teacher, own, chunks, blocks, count):
    toks, cols = logits.shape
    width = own.shape[0] * blocks
    vmem = pl.BlockSpec(memory_space=pltpu.VMEM)
    hbm = pl.BlockSpec(memory_space=pltpu.HBM)
    shape = (count, toks // 2, LANES)
    return pl.pallas_call(
        functools.partial(grad_kernel, blocks),
        out_shape=[
            jax.ShapeDtypeStruct(shape, jnp.float32),
            jax.ShapeDtypeStruct(shape, jnp.bfloat16),
            jax.ShapeDtypeStruct((1, toks), jnp.float32),
        ],
        in_specs=[pl.BlockSpec(memory_space=pltpu.SMEM)] + [vmem] * 2 + [hbm] * (3 + len(chunks)),
        out_specs=[vmem] * 3,
        scratch_shapes=[
            pltpu.VMEM((cols, toks), jnp.bfloat16),
            pltpu.VMEM((toks, cols), jnp.float32),
            pltpu.VMEM((toks, cols), jnp.bfloat16),
            pltpu.VMEM((len(chunks) + HALVES, own.shape[0] // HALVES, cols), jnp.bfloat16),
            pltpu.SemaphoreType.DMA((len(chunks) + HALVES + 2,)),
        ],
        compiler_params=pltpu.CompilerParams(vmem_limit_bytes=60 * 1024 * 1024),
        cost_estimate=pl.CostEstimate(
            flops=2 * toks * cols * width, bytes_accessed=2 * cols * width, transcendentals=toks * cols
        ),
    )(place, stats, weight, logits, teacher, own, *chunks)


def body(hidden, head, teacher_logits, lengths, slot_rollout, token_mask):
    tok_rows = hidden.shape[0]
    count = lax.axis_size("vocab")
    blocks = lax.axis_size("row")
    slot_count = tok_rows // WIN
    row_place = lax.axis_index("row")
    side_place = lax.axis_index("side")
    own_slots = lax.dynamic_slice_in_dim(slot_rollout, row_place * slot_count, slot_count)
    chosen = own_slots[:, None] == jnp.arange(lengths.shape[0], dtype=jnp.int32)[None, :]
    slot_length = jnp.sum(jnp.where(chosen, lengths[None, :], 0), axis=1)
    length_tok = jnp.repeat(slot_length, WIN)
    position = jnp.arange(tok_rows, dtype=jnp.int32) % WIN
    usable = (token_mask > 0) & (position < length_tok)
    weight = jnp.where(usable, 1.0 / length_tok.astype(jnp.float32), 0.0)

    full = head.shape[0]
    depth = full // HALVES
    ring = [(i, (i + 1) % blocks) for i in range(blocks)]
    ring += [(blocks + i, blocks + (i - 1) % blocks) for i in range(blocks)]
    step = 1 - 2 * side_place
    held = [head[part * depth : (part + 1) * depth] for part in range(HALVES)]
    logits = jnp.dot(
        lax.dynamic_slice_in_dim(hidden, row_place * full, full, axis=1), head, preferred_element_type=jnp.float32
    )
    chunks = []
    for distance in range(1, blocks):
        held = [lax.ppermute(part, ("side", "row"), ring) for part in held]
        owner = (row_place - distance * step + blocks) % blocks
        for part in range(HALVES):
            piece = lax.dynamic_slice_in_dim(hidden, owner * full + part * depth, depth, axis=1)
            logits = logits + jnp.dot(piece, held[part], preferred_element_type=jnp.float32)
        chunks += held

    teacher = teacher_logits.astype(jnp.float32)
    teacher_peak = jnp.max(teacher, axis=1)
    teacher_gap = teacher - teacher_peak[:, None]
    teacher_total = jnp.sum(jnp.exp(teacher_gap), axis=1)
    peak = jnp.max(logits, axis=1)
    shifted = logits - peak[:, None]
    powers = jnp.exp(shifted)
    total = jnp.sum(powers, axis=1)
    term = jnp.sum(powers * (shifted - teacher_gap), axis=1)
    blank = jnp.zeros_like(peak)
    own = jnp.stack([peak, total, teacher_peak, teacher_total, term, blank, blank, blank])
    other = swap_side(own)
    pair = jnp.concatenate([*join(*[jnp.stack([own[i], other[i]]) for i in range(5)]), own[5:]])
    stats = lax.all_to_all(jnp.broadcast_to(pair, (count,) + pair.shape), "vocab", 0, 0)

    place = jnp.stack([side_place, row_place]).astype(jnp.int32)
    keep, send, diverge = grad_products(
        place, stats, weight[None], logits, teacher_logits, head, chunks, blocks, count
    )
    packed = (keep + swap_side(send).astype(jnp.float32)).astype(jnp.bfloat16)
    pieces = lax.all_to_all(packed, "vocab", 0, 0)
    summed = jnp.sum(pieces.astype(jnp.float32), axis=0).astype(jnp.bfloat16)
    rest = tok_rows - LANES
    lower = jnp.concatenate([summed[64:, :rest], summed[64:, rest:]], axis=0)
    hidden_grad = jnp.concatenate([summed[:64], lower], axis=1).T
    slot_loss = jnp.sum((weight * diverge[0]).reshape(slot_count, WIN), axis=1)
    return (slot_loss, hidden_grad)


def solution(mesh):
    in_specs = (
        P("row", None),
        P("row", ("side", "vocab")),
        P("row", ("side", "vocab")),
        P(),
        P(),
        P("row"),
    )
    out_specs = (P("row"), P("row", ("side", "vocab")))
    return jax.shard_map(body, mesh=mesh, in_specs=in_specs, out_specs=out_specs, check_vma=False)
```

```python
import functools

import jax
import jax.numpy as jnp
from jax import lax
from jax.experimental import pallas as pl
from jax.experimental.pallas import tpu as pltpu
from jax.sharding import PartitionSpec as P

WIN = 16
HALVES = 2
LANES = 128


loss_scale = 256.0


def swap_side(value):
    return lax.ppermute(value, "side", [(0, 1), (1, 0)])


def join(peak, total, teacher_peak, teacher_total, term):
    top = jnp.max(peak, axis=0, keepdims=True)
    teacher_top = jnp.max(teacher_peak, axis=0, keepdims=True)
    shift = peak - top
    teacher_shift = teacher_peak - teacher_top
    scale = jnp.exp(shift)
    return (
        top,
        jnp.sum(total * scale, axis=0, keepdims=True),
        teacher_top,
        jnp.sum(teacher_total * jnp.exp(teacher_shift), axis=0, keepdims=True),
        jnp.sum(scale * (term + total * (shift - teacher_shift)), axis=0, keepdims=True),
    )


def grad_kernel(blocks, place_ref, stats_ref, weight_ref, logits_ref, teacher_ref, own_ref, *refs):
    chunk_refs = refs[:-8]
    keep_ref, send_ref, diverge_ref, grad_ref, logits_buf, teacher_buf, head_buf, sems = refs[-8:]
    side = place_ref[0]
    row = place_ref[1]
    step = 1 - 2 * side
    toks = logits_ref.shape[0]
    rest = toks - LANES
    depth = own_ref.shape[0] // HALVES
    copies = [
        pltpu.make_async_copy(logits_ref, logits_buf, sems.at[0]),
        pltpu.make_async_copy(teacher_ref, teacher_buf, sems.at[1]),
    ]
    sources = [own_ref.at[part * depth : (part + 1) * depth] for part in range(HALVES)] + list(chunk_refs)
    for index, source in enumerate(sources):
        copies.append(pltpu.make_async_copy(source, head_buf.at[index], sems.at[2 + index]))
    for copy in copies:
        copy.start()

    peak, total, teacher_peak, teacher_total, term = join(*[stats_ref[:, i, :] for i in range(5)])
    mean = term / total
    diverge_ref[...] = mean - jnp.log(total) + jnp.log(teacher_total)
    scale = loss_scale * weight_ref[...] / total
    offset = teacher_peak - mean
    table = jnp.concatenate([peak, scale, offset, jnp.zeros((LANES - 3, toks), jnp.float32)], axis=0)
    table = jnp.concatenate([table, jnp.zeros((LANES, 2 * LANES - toks), jnp.float32)], axis=1)
    columns = jnp.transpose(table)[:toks]
    copies[0].wait()
    copies[1].wait()
    shifted = logits_buf[...] - columns[:, 0:1]
    slope = shifted - teacher_buf[...].astype(jnp.float32) + columns[:, 2:3]
    grad = columns[:, 1:2] * jnp.exp(shifted) * slope
    grad_ref[...] = jnp.transpose(grad).astype(jnp.bfloat16)
    low = lax.broadcasted_iota(jnp.int32, (32, LANES), 1) < rest

    def one(product, distance, part):
        owner = lax.rem(row - distance * step + blocks, blocks)
        first = lax.rem(owner, blocks // 2) * (HALVES * depth // 64) + part * (depth // 64)
        mine = lax.div(owner, blocks // 2) == side
        wide = jnp.concatenate([product[:, LANES:], jnp.zeros((depth, LANES - rest), jnp.float32)], axis=1)
        pieces = []
        for i in range(depth // 64):
            left = wide[64 * i : 64 * i + 32]
            right = wide[64 * i + 32 : 64 * i + 64]
            pieces.append((product[64 * i : 64 * i + 64, :LANES], jnp.where(low, left, pltpu.roll(right, rest, 1))))

        @pl.when(mine)
        def _():
            for i, (upper, lower) in enumerate(pieces):
                keep_ref[first + i, :64] = upper
                keep_ref[first + i, 64:] = lower

        @pl.when(jnp.logical_not(mine))
        def _():
            for i, (upper, lower) in enumerate(pieces):
                send_ref[first + i, :64] = upper.astype(send_ref.dtype)
                send_ref[first + i, 64:] = lower.astype(send_ref.dtype)

    for base in range(0, len(sources), HALVES):
        for index in range(base, base + HALVES):
            copies[2 + index].wait()
        block = head_buf[base : base + HALVES].reshape(HALVES * depth, head_buf.shape[2])
        product = jnp.dot(block, grad_ref[...], preferred_element_type=jnp.float32)
        for part in range(HALVES):
            one(product[part * depth : (part + 1) * depth], base // HALVES, part)


def grad_products(place, stats, weight, logits, teacher, own, chunks, blocks, count):
    toks, cols = logits.shape
    width = own.shape[0] * blocks
    vmem = pl.BlockSpec(memory_space=pltpu.VMEM)
    hbm = pl.BlockSpec(memory_space=pltpu.HBM)
    shape = (count, toks // 2, LANES)
    large = [pltpu.with_memory_space_constraint(value, pltpu.HBM) for value in (logits, teacher, own, *chunks)]
    return pl.pallas_call(
        functools.partial(grad_kernel, blocks),
        out_shape=[
            jax.ShapeDtypeStruct(shape, jnp.float32),
            jax.ShapeDtypeStruct(shape, jnp.bfloat16),
            jax.ShapeDtypeStruct((1, toks), jnp.float32),
        ],
        in_specs=[pl.BlockSpec(memory_space=pltpu.SMEM)] + [vmem] * 2 + [hbm] * (3 + len(chunks)),
        out_specs=[vmem] * 3,
        scratch_shapes=[
            pltpu.VMEM((cols, toks), jnp.bfloat16),
            pltpu.VMEM((toks, cols), jnp.float32),
            pltpu.VMEM((toks, cols), jnp.bfloat16),
            pltpu.VMEM((len(chunks) + HALVES, own.shape[0] // HALVES, cols), jnp.bfloat16),
            pltpu.SemaphoreType.DMA((len(chunks) + HALVES + 2,)),
        ],
        compiler_params=pltpu.CompilerParams(vmem_limit_bytes=24 * 1024 * 1024),
        cost_estimate=pl.CostEstimate(
            flops=2 * toks * cols * width, bytes_accessed=2 * cols * width, transcendentals=toks * cols
        ),
    )(place, stats, weight, *large)


def body(hidden, head, teacher_logits, lengths, slot_rollout, token_mask):
    tok_rows = hidden.shape[0]
    count = lax.axis_size("vocab")
    blocks = lax.axis_size("row")
    slot_count = tok_rows // WIN
    row_place = lax.axis_index("row")
    side_place = lax.axis_index("side")
    own_slots = lax.dynamic_slice_in_dim(slot_rollout, row_place * slot_count, slot_count)
    chosen = own_slots[:, None] == jnp.arange(lengths.shape[0], dtype=jnp.int32)[None, :]
    slot_length = jnp.sum(jnp.where(chosen, lengths[None, :], 0), axis=1)
    length_tok = jnp.repeat(slot_length, WIN)
    position = jnp.arange(tok_rows, dtype=jnp.int32) % WIN
    usable = (token_mask > 0) & (position < length_tok)
    weight = jnp.where(usable, 1.0 / length_tok.astype(jnp.float32), 0.0)

    full = head.shape[0]
    depth = full // HALVES
    ring = [(i, (i + 1) % blocks) for i in range(blocks)]
    ring += [(blocks + i, blocks + (i - 1) % blocks) for i in range(blocks)]
    step = 1 - 2 * side_place
    held = [head[part * depth : (part + 1) * depth] for part in range(HALVES)]
    logits = jnp.dot(
        lax.dynamic_slice_in_dim(hidden, row_place * full, full, axis=1), head, preferred_element_type=jnp.float32
    )
    chunks = []
    for distance in range(1, blocks):
        held = [lax.ppermute(part, ("side", "row"), ring) for part in held]
        owner = (row_place - distance * step + blocks) % blocks
        for part in range(HALVES):
            piece = lax.dynamic_slice_in_dim(hidden, owner * full + part * depth, depth, axis=1)
            logits = logits + jnp.dot(piece, held[part], preferred_element_type=jnp.float32)
        chunks += held

    teacher = teacher_logits.astype(jnp.float32)
    teacher_peak = jnp.max(teacher, axis=1)
    teacher_gap = teacher - teacher_peak[:, None]
    teacher_total = jnp.sum(jnp.exp(teacher_gap), axis=1)
    peak = jnp.max(logits, axis=1)
    shifted = logits - peak[:, None]
    powers = jnp.exp(shifted)
    total = jnp.sum(powers, axis=1)
    term = jnp.sum(powers * (shifted - teacher_gap), axis=1)
    blank = jnp.zeros_like(peak)
    own = jnp.stack([peak, total, teacher_peak, teacher_total, term, blank, blank, blank])
    other = swap_side(own)
    pair = jnp.concatenate([*join(*[jnp.stack([own[i], other[i]]) for i in range(5)]), own[5:]])
    stats = lax.all_to_all(jnp.broadcast_to(pair, (count,) + pair.shape), "vocab", 0, 0)

    place = jnp.stack([side_place, row_place]).astype(jnp.int32)
    keep, send, diverge = grad_products(
        place, stats, weight[None], logits, teacher_logits, head, chunks, blocks, count
    )
    packed = (keep + swap_side(send).astype(jnp.float32)).astype(jnp.bfloat16)
    pieces = lax.all_to_all(packed, "vocab", 0, 0)
    summed = jnp.sum(pieces.astype(jnp.float32), axis=0).astype(jnp.bfloat16)
    rest = tok_rows - LANES
    lower = jnp.concatenate([summed[64:, :rest], summed[64:, rest:]], axis=0)
    hidden_grad = jnp.concatenate([summed[:64], lower], axis=1).T
    slot_loss = jnp.sum((weight * diverge[0]).reshape(slot_count, WIN), axis=1)
    return (slot_loss, hidden_grad)


def solution(mesh):
    in_specs = (
        P("row", None),
        P("row", ("side", "vocab")),
        P("row", ("side", "vocab")),
        P(),
        P(),
        P("row"),
    )
    out_specs = (P("row"), P("row", ("side", "vocab")))
    return jax.shard_map(body, mesh=mesh, in_specs=in_specs, out_specs=out_specs, check_vma=False)
```

```python
import functools

import jax
import jax.numpy as jnp
from jax import lax
from jax.experimental import pallas as pl
from jax.experimental.pallas import tpu as pltpu
from jax.sharding import PartitionSpec as P

WIN = 16
HALVES = 2
LANES = 128


loss_scale = 256.0


def swap_side(value):
    return lax.ppermute(value, "side", [(0, 1), (1, 0)])


def join(peak, total, teacher_peak, teacher_total, term):
    top = jnp.max(peak, axis=0, keepdims=True)
    teacher_top = jnp.max(teacher_peak, axis=0, keepdims=True)
    shift = peak - top
    teacher_shift = teacher_peak - teacher_top
    scale = jnp.exp(shift)
    return (
        top,
        jnp.sum(total * scale, axis=0, keepdims=True),
        teacher_top,
        jnp.sum(teacher_total * jnp.exp(teacher_shift), axis=0, keepdims=True),
        jnp.sum(scale * (term + total * (shift - teacher_shift)), axis=0, keepdims=True),
    )


def grad_kernel(blocks, place_ref, stats_ref, weight_ref, logits_ref, teacher_ref, own_ref, *refs):
    chunk_refs = refs[:-8]
    keep_ref, send_ref, diverge_ref, grad_ref, logits_buf, teacher_buf, head_buf, sems = refs[-8:]
    side = place_ref[0]
    row = place_ref[1]
    step = 1 - 2 * side
    toks = logits_ref.shape[0]
    rest = toks - LANES
    depth = own_ref.shape[0] // HALVES
    copies = [
        pltpu.make_async_copy(logits_ref, logits_buf, sems.at[0]),
        pltpu.make_async_copy(teacher_ref, teacher_buf, sems.at[1]),
    ]
    sources = [own_ref.at[part * depth : (part + 1) * depth] for part in range(HALVES)] + list(chunk_refs)
    for index, source in enumerate(sources):
        copies.append(pltpu.make_async_copy(source, head_buf.at[index], sems.at[2 + index]))
    for copy in copies:
        copy.start()

    peak, total, teacher_peak, teacher_total, term = join(*[stats_ref[:, i, :] for i in range(5)])
    mean = term / total
    diverge_ref[...] = mean - jnp.log(total) + jnp.log(teacher_total)
    scale = loss_scale * weight_ref[...] / total
    offset = teacher_peak - mean
    table = jnp.concatenate([peak, scale, offset, jnp.zeros((LANES - 3, toks), jnp.float32)], axis=0)
    table = jnp.concatenate([table, jnp.zeros((LANES, 2 * LANES - toks), jnp.float32)], axis=1)
    columns = jnp.transpose(table)[:toks]
    copies[0].wait()
    copies[1].wait()
    shifted = logits_buf[...] - columns[:, 0:1]
    slope = shifted - teacher_buf[...].astype(jnp.float32) + columns[:, 2:3]
    grad = columns[:, 1:2] * jnp.exp(shifted) * slope
    grad_ref[...] = jnp.transpose(grad).astype(jnp.bfloat16)
    low = lax.broadcasted_iota(jnp.int32, (32, LANES), 1) < rest

    def one(product, distance, part):
        owner = lax.rem(row - distance * step + blocks, blocks)
        first = lax.rem(owner, blocks // 2) * (HALVES * depth // 64) + part * (depth // 64)
        mine = lax.div(owner, blocks // 2) == side
        wide = jnp.concatenate([product[:, LANES:], jnp.zeros((depth, LANES - rest), jnp.float32)], axis=1)
        pieces = []
        for i in range(depth // 64):
            left = wide[64 * i : 64 * i + 32]
            right = wide[64 * i + 32 : 64 * i + 64]
            pieces.append((product[64 * i : 64 * i + 64, :LANES], jnp.where(low, left, pltpu.roll(right, rest, 1))))

        @pl.when(mine)
        def _():
            for i, (upper, lower) in enumerate(pieces):
                keep_ref[first + i, :64] = upper
                keep_ref[first + i, 64:] = lower

        @pl.when(jnp.logical_not(mine))
        def _():
            for i, (upper, lower) in enumerate(pieces):
                send_ref[first + i, :64] = upper.astype(send_ref.dtype)
                send_ref[first + i, 64:] = lower.astype(send_ref.dtype)

    for base in range(0, len(sources), HALVES):
        for index in range(base, base + HALVES):
            copies[2 + index].wait()
        block = head_buf[base : base + HALVES].reshape(HALVES * depth, head_buf.shape[2])
        product = jnp.dot(block, grad_ref[...], preferred_element_type=jnp.float32)
        for part in range(HALVES):
            one(product[part * depth : (part + 1) * depth], base // HALVES, part)


def grad_products(place, stats, weight, logits, teacher, own, chunks, blocks, count):
    toks, cols = logits.shape
    width = own.shape[0] * blocks
    vmem = pl.BlockSpec(memory_space=pltpu.VMEM)
    hbm = pl.BlockSpec(memory_space=pltpu.HBM)
    shape = (count, toks // 2, LANES)
    large = [pltpu.with_memory_space_constraint(value, pltpu.HBM) for value in (logits, teacher, own, *chunks)]
    return pl.pallas_call(
        functools.partial(grad_kernel, blocks),
        out_shape=[
            jax.ShapeDtypeStruct(shape, jnp.float32),
            jax.ShapeDtypeStruct(shape, jnp.bfloat16),
            jax.ShapeDtypeStruct((1, toks), jnp.float32),
        ],
        in_specs=[pl.BlockSpec(memory_space=pltpu.SMEM)] + [vmem] * 2 + [hbm] * (3 + len(chunks)),
        out_specs=[vmem] * 3,
        scratch_shapes=[
            pltpu.VMEM((cols, toks), jnp.bfloat16),
            pltpu.VMEM((toks, cols), jnp.float32),
            pltpu.VMEM((toks, cols), jnp.bfloat16),
            pltpu.VMEM((len(chunks) + HALVES, own.shape[0] // HALVES, cols), jnp.bfloat16),
            pltpu.SemaphoreType.DMA((len(chunks) + HALVES + 2,)),
        ],
        compiler_params=pltpu.CompilerParams(vmem_limit_bytes=24 * 1024 * 1024),
        cost_estimate=pl.CostEstimate(
            flops=2 * toks * cols * width, bytes_accessed=2 * cols * width, transcendentals=toks * cols
        ),
    )(place, stats, weight, *large)


def body(hidden, head, teacher_logits, lengths, slot_rollout, token_mask):
    tok_rows = hidden.shape[0]
    count = lax.axis_size("vocab")
    blocks = lax.axis_size("row")
    slot_count = tok_rows // WIN
    row_place = lax.axis_index("row")
    side_place = lax.axis_index("side")
    own_slots = lax.dynamic_slice_in_dim(slot_rollout, row_place * slot_count, slot_count)
    chosen = own_slots[:, None] == jnp.arange(lengths.shape[0], dtype=jnp.int32)[None, :]
    slot_length = jnp.sum(jnp.where(chosen, lengths[None, :], 0), axis=1)
    length_tok = jnp.repeat(slot_length, WIN)
    position = jnp.arange(tok_rows, dtype=jnp.int32) % WIN
    usable = (token_mask > 0) & (position < length_tok)
    weight = jnp.where(usable, 1.0 / length_tok.astype(jnp.float32), 0.0)

    full = head.shape[0]
    depth = full // HALVES
    ring = [(i, (i + 1) % blocks) for i in range(blocks)]
    ring += [(blocks + i, blocks + (i - 1) % blocks) for i in range(blocks)]
    step = 1 - 2 * side_place
    held = [head[part * depth : (part + 1) * depth] for part in range(HALVES)]
    logits = jnp.dot(
        lax.dynamic_slice_in_dim(hidden, row_place * full, full, axis=1), head, preferred_element_type=jnp.float32
    )
    chunks = []
    for distance in range(1, blocks):
        held = [lax.ppermute(part, ("side", "row"), ring) for part in held]
        owner = (row_place - distance * step + blocks) % blocks
        for part in range(HALVES):
            piece = lax.dynamic_slice_in_dim(hidden, owner * full + part * depth, depth, axis=1)
            logits = logits + jnp.dot(piece, held[part], preferred_element_type=jnp.float32)
        chunks += held

    teacher = teacher_logits.astype(jnp.float32)
    teacher_peak = jnp.max(teacher, axis=1)
    teacher_gap = teacher - teacher_peak[:, None]
    teacher_total = jnp.sum(jnp.exp(teacher_gap), axis=1)
    peak = jnp.max(logits, axis=1)
    shifted = logits - peak[:, None]
    powers = jnp.exp(shifted)
    total = jnp.sum(powers, axis=1)
    term = jnp.sum(powers * (shifted - teacher_gap), axis=1)
    blank = jnp.zeros_like(peak)
    own = jnp.stack([peak, total, teacher_peak, teacher_total, term, blank, blank, blank])
    stats = lax.all_to_all(jnp.broadcast_to(own, (2 * count,) + own.shape), ("side", "vocab"), 0, 0)

    place = jnp.stack([side_place, row_place]).astype(jnp.int32)
    keep, send, diverge = grad_products(
        place, stats, weight[None], logits, teacher_logits, head, chunks, blocks, count
    )
    packed = (keep + swap_side(send).astype(jnp.float32)).astype(jnp.bfloat16)
    pieces = lax.all_to_all(packed, "vocab", 0, 0)
    summed = jnp.sum(pieces.astype(jnp.float32), axis=0).astype(jnp.bfloat16)
    rest = tok_rows - LANES
    lower = jnp.concatenate([summed[64:, :rest], summed[64:, rest:]], axis=0)
    hidden_grad = jnp.concatenate([summed[:64], lower], axis=1).T
    slot_loss = jnp.sum((weight * diverge[0]).reshape(slot_count, WIN), axis=1)
    return (slot_loss, hidden_grad)


def solution(mesh):
    in_specs = (
        P("row", None),
        P("row", ("side", "vocab")),
        P("row", ("side", "vocab")),
        P(),
        P(),
        P("row"),
    )
    out_specs = (P("row"), P("row", ("side", "vocab")))
    return jax.shard_map(body, mesh=mesh, in_specs=in_specs, out_specs=out_specs, check_vma=False)
```

```python
import functools

import jax
import jax.numpy as jnp
from jax import lax
from jax.experimental import pallas as pl
from jax.experimental.pallas import tpu as pltpu
from jax.sharding import PartitionSpec as P

WIN = 16
HALVES = 2
LANES = 128


loss_scale = 256.0


def swap_side(value):
    return lax.ppermute(value, "side", [(0, 1), (1, 0)])


def join(peak, total, teacher_peak, teacher_total, term):
    top = jnp.max(peak, axis=0, keepdims=True)
    teacher_top = jnp.max(teacher_peak, axis=0, keepdims=True)
    shift = peak - top
    teacher_shift = teacher_peak - teacher_top
    scale = jnp.exp(shift)
    return (
        top,
        jnp.sum(total * scale, axis=0, keepdims=True),
        teacher_top,
        jnp.sum(teacher_total * jnp.exp(teacher_shift), axis=0, keepdims=True),
        jnp.sum(scale * (term + total * (shift - teacher_shift)), axis=0, keepdims=True),
    )


def grad_kernel(blocks, place_ref, stats_ref, weight_ref, logits_ref, teacher_ref, own_ref, *refs):
    chunk_refs = refs[:-8]
    keep_ref, send_ref, diverge_ref, grad_ref, logits_buf, teacher_buf, head_buf, sems = refs[-8:]
    side = place_ref[0]
    row = place_ref[1]
    step = 1 - 2 * side
    toks = logits_ref.shape[0]
    rest = toks - LANES
    depth = own_ref.shape[0] // HALVES
    copies = [
        pltpu.make_async_copy(logits_ref, logits_buf, sems.at[0]),
        pltpu.make_async_copy(teacher_ref, teacher_buf, sems.at[1]),
    ]
    sources = [own_ref.at[part * depth : (part + 1) * depth] for part in range(HALVES)] + list(chunk_refs)
    for index, source in enumerate(sources):
        copies.append(pltpu.make_async_copy(source, head_buf.at[index], sems.at[2 + index]))
    for copy in copies:
        copy.start()

    peak, total, teacher_peak, teacher_total, term = join(*[stats_ref[:, i, :] for i in range(5)])
    mean = term / total
    diverge_ref[...] = mean - jnp.log(total) + jnp.log(teacher_total)
    scale = loss_scale * weight_ref[...] / total
    offset = teacher_peak - mean
    table = jnp.concatenate([peak, scale, offset, jnp.zeros((LANES - 3, toks), jnp.float32)], axis=0)
    table = jnp.concatenate([table, jnp.zeros((LANES, 2 * LANES - toks), jnp.float32)], axis=1)
    columns = jnp.transpose(table)[:toks]
    copies[0].wait()
    copies[1].wait()
    shifted = logits_buf[...] - columns[:, 0:1]
    slope = shifted - teacher_buf[...].astype(jnp.float32) + columns[:, 2:3]
    grad = columns[:, 1:2] * jnp.exp(shifted) * slope
    grad_ref[...] = jnp.transpose(grad).astype(jnp.bfloat16)
    low = lax.broadcasted_iota(jnp.int32, (32, LANES), 1) < rest

    def one(product, distance, part):
        owner = lax.rem(row - distance * step + blocks, blocks)
        first = lax.rem(owner, blocks // 2) * (HALVES * depth // 64) + part * (depth // 64)
        mine = lax.div(owner, blocks // 2) == side
        wide = jnp.concatenate([product[:, LANES:], jnp.zeros((depth, LANES - rest), jnp.float32)], axis=1)
        pieces = []
        for i in range(depth // 64):
            left = wide[64 * i : 64 * i + 32]
            right = wide[64 * i + 32 : 64 * i + 64]
            pieces.append((product[64 * i : 64 * i + 64, :LANES], jnp.where(low, left, pltpu.roll(right, rest, 1))))

        @pl.when(mine)
        def _():
            for i, (upper, lower) in enumerate(pieces):
                keep_ref[first + i, :64] = upper
                keep_ref[first + i, 64:] = lower

        @pl.when(jnp.logical_not(mine))
        def _():
            for i, (upper, lower) in enumerate(pieces):
                send_ref[first + i, :64] = upper.astype(send_ref.dtype)
                send_ref[first + i, 64:] = lower.astype(send_ref.dtype)

    for base in range(0, len(sources), HALVES):
        for index in range(base, base + HALVES):
            copies[2 + index].wait()
        block = head_buf[base : base + HALVES].reshape(HALVES * depth, head_buf.shape[2])
        product = jnp.dot(block, grad_ref[...], preferred_element_type=jnp.float32)
        for part in range(HALVES):
            one(product[part * depth : (part + 1) * depth], base // HALVES, part)


def grad_products(place, stats, weight, logits, teacher, own, chunks, blocks, count):
    toks, cols = logits.shape
    width = own.shape[0] * blocks
    vmem = pl.BlockSpec(memory_space=pltpu.VMEM)
    hbm = pl.BlockSpec(memory_space=pltpu.HBM)
    shape = (count, toks // 2, LANES)
    large = [pltpu.with_memory_space_constraint(value, pltpu.HBM) for value in (logits, teacher, own, *chunks)]
    return pl.pallas_call(
        functools.partial(grad_kernel, blocks),
        out_shape=[
            jax.ShapeDtypeStruct(shape, jnp.float32),
            jax.ShapeDtypeStruct(shape, jnp.bfloat16),
            jax.ShapeDtypeStruct((1, toks), jnp.float32),
        ],
        in_specs=[pl.BlockSpec(memory_space=pltpu.SMEM)] + [vmem] * 2 + [hbm] * (3 + len(chunks)),
        out_specs=[vmem] * 3,
        scratch_shapes=[
            pltpu.VMEM((cols, toks), jnp.bfloat16),
            pltpu.VMEM((toks, cols), jnp.float32),
            pltpu.VMEM((toks, cols), jnp.bfloat16),
            pltpu.VMEM((len(chunks) + HALVES, own.shape[0] // HALVES, cols), jnp.bfloat16),
            pltpu.SemaphoreType.DMA((len(chunks) + HALVES + 2,)),
        ],
        compiler_params=pltpu.CompilerParams(vmem_limit_bytes=24 * 1024 * 1024),
        cost_estimate=pl.CostEstimate(
            flops=2 * toks * cols * width, bytes_accessed=2 * cols * width, transcendentals=toks * cols
        ),
    )(place, stats, weight, *large)


def body(hidden, head, teacher_logits, lengths, slot_rollout, token_mask):
    tok_rows = hidden.shape[0]
    count = lax.axis_size("vocab")
    blocks = lax.axis_size("row")
    slot_count = tok_rows // WIN
    row_place = lax.axis_index("row")
    side_place = lax.axis_index("side")
    own_slots = lax.dynamic_slice_in_dim(slot_rollout, row_place * slot_count, slot_count)
    chosen = own_slots[:, None] == jnp.arange(lengths.shape[0], dtype=jnp.int32)[None, :]
    slot_length = jnp.sum(jnp.where(chosen, lengths[None, :], 0), axis=1)
    length_tok = jnp.repeat(slot_length, WIN)
    position = jnp.arange(tok_rows, dtype=jnp.int32) % WIN
    usable = (token_mask > 0) & (position < length_tok)
    weight = jnp.where(usable, 1.0 / length_tok.astype(jnp.float32), 0.0)

    full = head.shape[0]
    depth = full // HALVES
    ring = [(i, (i + 1) % blocks) for i in range(blocks)]
    ring += [(blocks + i, blocks + (i - 1) % blocks) for i in range(blocks)]
    step = 1 - 2 * side_place
    held = [head[part * depth : (part + 1) * depth] for part in range(HALVES)]
    logits = jnp.dot(
        lax.dynamic_slice_in_dim(hidden, row_place * full, full, axis=1), head, preferred_element_type=jnp.float32
    )
    chunks = []

    def add(logits, distance, part):
        owner = (row_place - distance * step + blocks) % blocks
        piece = lax.dynamic_slice_in_dim(hidden, owner * full + part * depth, depth, axis=1)
        return logits + jnp.dot(piece, held[part], preferred_element_type=jnp.float32)

    for distance in range(1, blocks):
        for part in range(HALVES):
            arrived = lax.ppermute(held[part], ("side", "row"), ring)
            if distance > 1:
                logits = add(logits, distance - 1, part)
            held[part], logits = lax.optimization_barrier((arrived, logits))
        chunks += held
    for part in range(HALVES):
        logits = add(logits, blocks - 1, part)

    teacher = teacher_logits.astype(jnp.float32)
    teacher_peak = jnp.max(teacher, axis=1)
    teacher_gap = teacher - teacher_peak[:, None]
    teacher_total = jnp.sum(jnp.exp(teacher_gap), axis=1)
    peak = jnp.max(logits, axis=1)
    shifted = logits - peak[:, None]
    powers = jnp.exp(shifted)
    total = jnp.sum(powers, axis=1)
    term = jnp.sum(powers * (shifted - teacher_gap), axis=1)
    blank = jnp.zeros_like(peak)
    own = jnp.stack([peak, total, teacher_peak, teacher_total, term, blank, blank, blank])
    other = swap_side(own)
    pair = jnp.concatenate([*join(*[jnp.stack([own[i], other[i]]) for i in range(5)]), own[5:]])
    stats = lax.all_to_all(jnp.broadcast_to(pair, (count,) + pair.shape), "vocab", 0, 0)

    place = jnp.stack([side_place, row_place]).astype(jnp.int32)
    keep, send, diverge = grad_products(
        place, stats, weight[None], logits, teacher_logits, head, chunks, blocks, count
    )
    packed = (keep + swap_side(send).astype(jnp.float32)).astype(jnp.bfloat16)
    pieces = lax.all_to_all(packed, "vocab", 0, 0)
    summed = jnp.sum(pieces.astype(jnp.float32), axis=0).astype(jnp.bfloat16)
    rest = tok_rows - LANES
    lower = jnp.concatenate([summed[64:, :rest], summed[64:, rest:]], axis=0)
    hidden_grad = jnp.concatenate([summed[:64], lower], axis=1).T
    slot_loss = jnp.sum((weight * diverge[0]).reshape(slot_count, WIN), axis=1)
    return (slot_loss, hidden_grad)


def solution(mesh):
    in_specs = (
        P("row", None),
        P("row", ("side", "vocab")),
        P("row", ("side", "vocab")),
        P(),
        P(),
        P("row"),
    )
    out_specs = (P("row"), P("row", ("side", "vocab")))
    return jax.shard_map(body, mesh=mesh, in_specs=in_specs, out_specs=out_specs, check_vma=False)
```

```python
import functools

import jax
import jax.numpy as jnp
from jax import lax
from jax.experimental import pallas as pl
from jax.experimental.pallas import tpu as pltpu
from jax.sharding import PartitionSpec as P

WIN = 16
HALVES = 2
WAITED = 4
LANES = 128


loss_scale = 256.0


def swap_side(value):
    return lax.ppermute(value, "side", [(0, 1), (1, 0)])


def join(peak, total, teacher_peak, teacher_total, term):
    top = jnp.max(peak, axis=0, keepdims=True)
    teacher_top = jnp.max(teacher_peak, axis=0, keepdims=True)
    shift = peak - top
    teacher_shift = teacher_peak - teacher_top
    scale = jnp.exp(shift)
    return (
        top,
        jnp.sum(total * scale, axis=0, keepdims=True),
        teacher_top,
        jnp.sum(teacher_total * jnp.exp(teacher_shift), axis=0, keepdims=True),
        jnp.sum(scale * (term + total * (shift - teacher_shift)), axis=0, keepdims=True),
    )


def grad_kernel(blocks, place_ref, stats_ref, weight_ref, logits_ref, teacher_ref, own_ref, *refs):
    chunk_refs = refs[:-8]
    sums_ref, send_ref, diverge_ref, grad_ref, logits_buf, teacher_buf, head_buf, sems = refs[-8:]
    side = place_ref[0]
    row = place_ref[1]
    step = 1 - 2 * side
    toks = logits_ref.shape[0]
    rest = toks - LANES
    depth = own_ref.shape[0] // HALVES
    copies = [
        pltpu.make_async_copy(logits_ref, logits_buf, sems.at[0]),
        pltpu.make_async_copy(teacher_ref, teacher_buf, sems.at[1]),
    ]
    sources = [own_ref.at[part * depth : (part + 1) * depth] for part in range(HALVES)] + list(chunk_refs)
    for index, source in enumerate(sources):
        copies.append(pltpu.make_async_copy(source, head_buf.at[index], sems.at[2 + index]))
    for copy in copies:
        copy.start()

    peak, total, teacher_peak, teacher_total, term = join(*[stats_ref[:, i, :] for i in range(5)])
    mean = term / total
    diverge_ref[...] = mean - jnp.log(total) + jnp.log(teacher_total)
    scale = loss_scale * weight_ref[...] / total
    offset = teacher_peak - mean
    table = jnp.concatenate([peak, scale, offset, jnp.zeros((LANES - 3, toks), jnp.float32)], axis=0)
    table = jnp.concatenate([table, jnp.zeros((LANES, 2 * LANES - toks), jnp.float32)], axis=1)
    columns = jnp.transpose(table)[:toks]
    copies[0].wait()
    copies[1].wait()
    shifted = logits_buf[...] - columns[:, 0:1]
    slope = shifted - teacher_buf[...].astype(jnp.float32) + columns[:, 2:3]
    grad = columns[:, 1:2] * jnp.exp(shifted) * slope
    grad_ref[...] = jnp.transpose(grad).astype(jnp.bfloat16)
    low = lax.broadcasted_iota(jnp.int32, (32, LANES), 1) < rest

    def one(product, distance, part):
        owner = lax.rem(row - distance * step + blocks, blocks)
        first = lax.rem(owner, blocks // 2) * (HALVES * depth // 64) + part * (depth // 64)
        place = lax.rem(lax.div(owner, blocks // 2) + side, 2)
        wide = jnp.concatenate([product[:, LANES:], jnp.zeros((depth, LANES - rest), jnp.float32)], axis=1)
        for i in range(depth // 64):
            left = wide[64 * i : 64 * i + 32]
            right = wide[64 * i + 32 : 64 * i + 64]
            sums_ref[place, first + i, :64] = product[64 * i : 64 * i + 64, :LANES]
            sums_ref[place, first + i, 64:] = jnp.where(low, left, pltpu.roll(right, rest, 1))

    for base in range(0, len(sources), WAITED):
        for index in range(base, base + WAITED):
            copies[2 + index].wait()
        for index in range(base, base + WAITED):
            product = jnp.dot(head_buf[index], grad_ref[...], preferred_element_type=jnp.float32)
            one(product, index // HALVES, index % HALVES)
    send_ref[...] = sums_ref[1].astype(send_ref.dtype)


def grad_products(place, stats, weight, logits, teacher, own, chunks, blocks, count):
    toks, cols = logits.shape
    width = own.shape[0] * blocks
    vmem = pl.BlockSpec(memory_space=pltpu.VMEM)
    hbm = pl.BlockSpec(memory_space=pltpu.HBM)
    shape = (count, toks // 2, LANES)
    large = [pltpu.with_memory_space_constraint(value, pltpu.HBM) for value in (logits, teacher, own, *chunks)]
    return pl.pallas_call(
        functools.partial(grad_kernel, blocks),
        out_shape=[
            jax.ShapeDtypeStruct((2,) + shape, jnp.float32),
            jax.ShapeDtypeStruct(shape, jnp.bfloat16),
            jax.ShapeDtypeStruct((1, toks), jnp.float32),
        ],
        in_specs=[pl.BlockSpec(memory_space=pltpu.SMEM)] + [vmem] * 2 + [hbm] * (3 + len(chunks)),
        out_specs=[vmem] * 3,
        scratch_shapes=[
            pltpu.VMEM((cols, toks), jnp.bfloat16),
            pltpu.VMEM((toks, cols), jnp.float32),
            pltpu.VMEM((toks, cols), jnp.bfloat16),
            pltpu.VMEM((len(chunks) + HALVES, own.shape[0] // HALVES, cols), jnp.bfloat16),
            pltpu.SemaphoreType.DMA((len(chunks) + HALVES + 2,)),
        ],
        compiler_params=pltpu.CompilerParams(vmem_limit_bytes=24 * 1024 * 1024),
        cost_estimate=pl.CostEstimate(
            flops=2 * toks * cols * width, bytes_accessed=2 * cols * width, transcendentals=toks * cols
        ),
    )(place, stats, weight, *large)


def body(hidden, head, teacher_logits, lengths, slot_rollout, token_mask):
    tok_rows = hidden.shape[0]
    count = lax.axis_size("vocab")
    blocks = lax.axis_size("row")
    slot_count = tok_rows // WIN
    row_place = lax.axis_index("row")
    side_place = lax.axis_index("side")
    own_slots = lax.dynamic_slice_in_dim(slot_rollout, row_place * slot_count, slot_count)
    chosen = own_slots[:, None] == jnp.arange(lengths.shape[0], dtype=jnp.int32)[None, :]
    slot_length = jnp.sum(jnp.where(chosen, lengths[None, :], 0), axis=1)
    length_tok = jnp.repeat(slot_length, WIN)
    position = jnp.arange(tok_rows, dtype=jnp.int32) % WIN
    usable = (token_mask > 0) & (position < length_tok)
    weight = jnp.where(usable, 1.0 / length_tok.astype(jnp.float32), 0.0)

    full = head.shape[0]
    depth = full // HALVES
    ring = [(i, (i + 1) % blocks) for i in range(blocks)]
    ring += [(blocks + i, blocks + (i - 1) % blocks) for i in range(blocks)]
    step = 1 - 2 * side_place
    held = [head[part * depth : (part + 1) * depth] for part in range(HALVES)]
    logits = jnp.dot(
        lax.dynamic_slice_in_dim(hidden, row_place * full, full, axis=1), head, preferred_element_type=jnp.float32
    )
    chunks = []
    for distance in range(1, blocks):
        held = [lax.ppermute(part, ("side", "row"), ring) for part in held]
        owner = (row_place - distance * step + blocks) % blocks
        for part in range(HALVES):
            piece = lax.dynamic_slice_in_dim(hidden, owner * full + part * depth, depth, axis=1)
            logits = logits + jnp.dot(piece, held[part], preferred_element_type=jnp.float32)
        chunks += held

    teacher = teacher_logits.astype(jnp.float32)
    teacher_peak = jnp.max(teacher, axis=1)
    teacher_gap = teacher - teacher_peak[:, None]
    teacher_total = jnp.sum(jnp.exp(teacher_gap), axis=1)
    peak = jnp.max(logits, axis=1)
    shifted = logits - peak[:, None]
    powers = jnp.exp(shifted)
    total = jnp.sum(powers, axis=1)
    term = jnp.sum(powers * (shifted - teacher_gap), axis=1)
    blank = jnp.zeros_like(peak)
    own = jnp.stack([peak, total, teacher_peak, teacher_total, term, blank, blank, blank])
    other = swap_side(own)
    pair = jnp.concatenate([*join(*[jnp.stack([own[i], other[i]]) for i in range(5)]), own[5:]])
    stats = lax.all_to_all(jnp.broadcast_to(pair, (count,) + pair.shape), "vocab", 0, 0)

    place = jnp.stack([side_place, row_place]).astype(jnp.int32)
    sums, send, diverge = grad_products(
        place, stats, weight[None], logits, teacher_logits, head, chunks, blocks, count
    )
    packed = (sums[0] + swap_side(send).astype(jnp.float32)).astype(jnp.bfloat16)
    pieces = lax.all_to_all(packed, "vocab", 0, 0)
    summed = jnp.sum(pieces.astype(jnp.float32), axis=0).astype(jnp.bfloat16)
    rest = tok_rows - LANES
    lower = jnp.concatenate([summed[64:, :rest], summed[64:, rest:]], axis=0)
    hidden_grad = jnp.concatenate([summed[:64], lower], axis=1).T
    slot_loss = jnp.sum((weight * diverge[0]).reshape(slot_count, WIN), axis=1)
    return (slot_loss, hidden_grad)


def solution(mesh):
    in_specs = (
        P("row", None),
        P("row", ("side", "vocab")),
        P("row", ("side", "vocab")),
        P(),
        P(),
        P("row"),
    )
    out_specs = (P("row"), P("row", ("side", "vocab")))
    return jax.shard_map(body, mesh=mesh, in_specs=in_specs, out_specs=out_specs, check_vma=False)
```

```python
import functools

import jax
import jax.numpy as jnp
from jax import lax
from jax.experimental import pallas as pl
from jax.experimental.pallas import tpu as pltpu
from jax.sharding import PartitionSpec as P

WIN = 16
HALVES = 2
WAITED = 4
FEW = 144
LANES = 128


loss_scale = 256.0


def swap_side(value):
    return lax.ppermute(value, "side", [(0, 1), (1, 0)])


def join(peak, total, teacher_peak, teacher_total, term):
    top = jnp.max(peak, axis=0, keepdims=True)
    teacher_top = jnp.max(teacher_peak, axis=0, keepdims=True)
    shift = peak - top
    teacher_shift = teacher_peak - teacher_top
    scale = jnp.exp(shift)
    return (
        top,
        jnp.sum(total * scale, axis=0, keepdims=True),
        teacher_top,
        jnp.sum(teacher_total * jnp.exp(teacher_shift), axis=0, keepdims=True),
        jnp.sum(scale * (term + total * (shift - teacher_shift)), axis=0, keepdims=True),
    )


def grad_kernel(blocks, toks, place_ref, stats_ref, weight_ref, logits_ref, teacher_ref, own_ref, *refs):
    chunk_refs = refs[:-6]
    sums_ref, send_ref, diverge_ref, grad_ref, head_buf, sems = refs[-6:]
    side = place_ref[0]
    row = place_ref[1]
    step = 1 - 2 * side
    rest = toks - LANES
    groups = LANES // rest
    rows = 64 // groups
    depth = own_ref.shape[0] // HALVES
    sources = [own_ref.at[part * depth : (part + 1) * depth] for part in range(HALVES)] + list(chunk_refs)
    copies = [
        pltpu.make_async_copy(source, head_buf.at[index], sems.at[index]) for index, source in enumerate(sources)
    ]
    for copy in copies:
        copy.start()

    peak, total, teacher_peak, teacher_total, term = join(*[stats_ref[:, i, :toks] for i in range(5)])
    mean = term / total
    diverge_ref[...] = mean - jnp.log(total) + jnp.log(teacher_total)
    scale = loss_scale * weight_ref[:, :toks] / total
    offset = teacher_peak - mean
    table = jnp.concatenate([peak, scale, offset, jnp.zeros((LANES - 3, toks), jnp.float32)], axis=0)
    table = jnp.concatenate([table, jnp.zeros((LANES, 2 * LANES - toks), jnp.float32)], axis=1)
    columns = jnp.transpose(table)[:toks]
    shifted = logits_ref[:toks] - columns[:, 0:1]
    slope = shifted - teacher_ref[:toks].astype(jnp.float32) + columns[:, 2:3]
    grad = columns[:, 1:2] * jnp.exp(shifted) * slope
    grad_ref[...] = jnp.transpose(grad).astype(jnp.bfloat16)
    group = lax.broadcasted_iota(jnp.int32, (rows, LANES), 1) // rest

    def one(product, distance, part):
        owner = lax.rem(row - distance * step + blocks, blocks)
        first = lax.rem(owner, blocks // 2) * (HALVES * depth // 64) + part * (depth // 64)
        place = lax.rem(lax.div(owner, blocks // 2) + side, 2)
        wide = jnp.concatenate([product[:, LANES:], jnp.zeros((depth, LANES - rest), jnp.float32)], axis=1)
        for i in range(depth // 64):
            lower = wide[64 * i : 64 * i + rows]
            for near in range(1, groups):
                start = 64 * i + near * rows
                lower = jnp.where(group == near, pltpu.roll(wide[start : start + rows], near * rest, 1), lower)
            sums_ref[place, first + i, :64] = product[64 * i : 64 * i + 64, :LANES]
            sums_ref[place, first + i, 64:] = lower

    for base in range(0, len(sources), WAITED):
        for index in range(base, base + WAITED):
            copies[index].wait()
        for index in range(base, base + WAITED):
            product = jnp.dot(head_buf[index], grad_ref[...], preferred_element_type=jnp.float32)
            one(product, index // HALVES, index % HALVES)
    send_ref[...] = sums_ref[1].astype(send_ref.dtype)


def grad_products(place, stats, weight, logits, teacher, own, chunks, blocks, count, toks):
    cols = logits.shape[1]
    width = own.shape[0] * blocks
    vmem = pl.BlockSpec(memory_space=pltpu.VMEM)
    hbm = pl.BlockSpec(memory_space=pltpu.HBM)
    shape = (count, toks // 2, LANES)
    large = [pltpu.with_memory_space_constraint(value, pltpu.HBM) for value in (own, *chunks)]
    return pl.pallas_call(
        functools.partial(grad_kernel, blocks, toks),
        out_shape=[
            jax.ShapeDtypeStruct((2,) + shape, jnp.float32),
            jax.ShapeDtypeStruct(shape, jnp.bfloat16),
            jax.ShapeDtypeStruct((1, toks), jnp.float32),
        ],
        in_specs=[pl.BlockSpec(memory_space=pltpu.SMEM)] + [vmem] * 4 + [hbm] * (1 + len(chunks)),
        out_specs=[vmem] * 3,
        scratch_shapes=[
            pltpu.VMEM((cols, toks), jnp.bfloat16),
            pltpu.VMEM((len(chunks) + HALVES, own.shape[0] // HALVES, cols), jnp.bfloat16),
            pltpu.SemaphoreType.DMA((len(chunks) + HALVES,)),
        ],
        compiler_params=pltpu.CompilerParams(vmem_limit_bytes=24 * 1024 * 1024),
        cost_estimate=pl.CostEstimate(
            flops=2 * toks * cols * width, bytes_accessed=2 * cols * width, transcendentals=toks * cols
        ),
    )(place, stats, weight, logits, teacher, *large)


def body(hidden, head, teacher_logits, lengths, slot_rollout, token_mask):
    tok_rows = hidden.shape[0]
    count = lax.axis_size("vocab")
    blocks = lax.axis_size("row")
    slot_count = tok_rows // WIN
    row_place = lax.axis_index("row")
    side_place = lax.axis_index("side")
    chosen = slot_rollout[:, None] == jnp.arange(lengths.shape[0], dtype=jnp.int32)[None, :]
    all_lengths = jnp.sum(jnp.where(chosen, lengths[None, :], 0), axis=1)
    slot_length = lax.dynamic_slice_in_dim(all_lengths, row_place * slot_count, slot_count)
    length_tok = jnp.repeat(slot_length, WIN)
    token = jnp.arange(tok_rows, dtype=jnp.int32)
    inside = token % WIN < length_tok
    weight = jnp.where((token_mask > 0) & inside, 1.0 / length_tok.astype(jnp.float32), 0.0)

    earlier = token[None, :] < token[:, None]
    rank = jnp.sum((earlier & inside[None, :]).astype(jnp.int32), axis=1)
    spot = jnp.where(inside, rank, jnp.sum(inside.astype(jnp.int32)) + token - rank)
    pick = spot[None, :] == token[:, None]
    pick_low = pick.astype(jnp.bfloat16)
    hidden = jnp.dot(pick_low, hidden, preferred_element_type=jnp.float32).astype(jnp.bfloat16)
    teacher_logits = jnp.dot(pick_low, teacher_logits, preferred_element_type=jnp.float32).astype(jnp.bfloat16)
    weight = jnp.sum(jnp.where(pick, weight[None, :], 0.0), axis=1)
    fits = jnp.max(jnp.sum(all_lengths.reshape(blocks, slot_count), axis=1)) <= FEW

    full = head.shape[0]
    depth = full // HALVES
    ring = [(i, (i + 1) % blocks) for i in range(blocks)]
    ring += [(blocks + i, blocks + (i - 1) % blocks) for i in range(blocks)]
    step = 1 - 2 * side_place
    held = [head[part * depth : (part + 1) * depth] for part in range(HALVES)]
    logits = jnp.dot(
        lax.dynamic_slice_in_dim(hidden, row_place * full, full, axis=1), head, preferred_element_type=jnp.float32
    )
    chunks = []
    for distance in range(1, blocks):
        held = [lax.ppermute(part, ("side", "row"), ring) for part in held]
        owner = (row_place - distance * step + blocks) % blocks
        for part in range(HALVES):
            piece = lax.dynamic_slice_in_dim(hidden, owner * full + part * depth, depth, axis=1)
            logits = logits + jnp.dot(piece, held[part], preferred_element_type=jnp.float32)
        chunks += held

    teacher = teacher_logits.astype(jnp.float32)
    teacher_peak = jnp.max(teacher, axis=1)
    teacher_gap = teacher - teacher_peak[:, None]
    teacher_total = jnp.sum(jnp.exp(teacher_gap), axis=1)
    peak = jnp.max(logits, axis=1)
    shifted = logits - peak[:, None]
    powers = jnp.exp(shifted)
    total = jnp.sum(powers, axis=1)
    term = jnp.sum(powers * (shifted - teacher_gap), axis=1)
    blank = jnp.zeros_like(peak)
    own = jnp.stack([peak, total, teacher_peak, teacher_total, term, blank, blank, blank])
    other = swap_side(own)
    pair = jnp.concatenate([*join(*[jnp.stack([own[i], other[i]]) for i in range(5)]), own[5:]])
    stats = lax.all_to_all(jnp.broadcast_to(pair, (count,) + pair.shape), "vocab", 0, 0)

    place = jnp.stack([side_place, row_place]).astype(jnp.int32)

    def finish(toks, place, stats, weight, pick, logits, teacher_logits, head, *chunks):
        sums, send, diverge = grad_products(
            place, stats, weight[None], logits, teacher_logits, head, chunks, blocks, count, toks
        )
        packed = (sums[0] + swap_side(send).astype(jnp.float32)).astype(jnp.bfloat16)
        pieces = lax.all_to_all(packed, "vocab", 0, 0)
        summed = jnp.sum(pieces.astype(jnp.float32), axis=0).astype(jnp.bfloat16)
        rest = toks - LANES
        lower = jnp.concatenate([summed[64:, i : i + rest] for i in range(0, LANES, rest)], axis=0)
        block = jnp.concatenate([summed[:64], lower], axis=1)
        some = pick[:toks]
        block = jnp.dot(block, some.astype(jnp.bfloat16), preferred_element_type=jnp.float32).astype(jnp.bfloat16)
        loss = jnp.sum(jnp.where(some, (weight[:toks] * diverge[0])[:, None], 0.0), axis=0)
        return jnp.sum(loss.reshape(slot_count, WIN), axis=1), block.T

    stats, weight, pick = lax.optimization_barrier((stats, weight, pick))
    return lax.cond(
        fits,
        functools.partial(finish, FEW),
        functools.partial(finish, tok_rows),
        place, stats, weight, pick, logits, teacher_logits, head, *chunks,
    )


def solution(mesh):
    in_specs = (
        P("row", None),
        P("row", ("side", "vocab")),
        P("row", ("side", "vocab")),
        P(),
        P(),
        P("row"),
    )
    out_specs = (P("row"), P("row", ("side", "vocab")))
    return jax.shard_map(body, mesh=mesh, in_specs=in_specs, out_specs=out_specs, check_vma=False)
```

```python
import functools

import jax
import jax.numpy as jnp
from jax import lax
from jax.experimental import pallas as pl
from jax.experimental.pallas import tpu as pltpu
from jax.sharding import PartitionSpec as P

WIN = 16
HALVES = 2
WAITED = 4
FEW = 128
LANES = 128


loss_scale = 256.0


def swap_side(value):
    return lax.ppermute(value, "side", [(0, 1), (1, 0)])


def join(peak, total, teacher_peak, teacher_total, term):
    top = jnp.max(peak, axis=0, keepdims=True)
    teacher_top = jnp.max(teacher_peak, axis=0, keepdims=True)
    shift = peak - top
    teacher_shift = teacher_peak - teacher_top
    scale = jnp.exp(shift)
    return (
        top,
        jnp.sum(total * scale, axis=0, keepdims=True),
        teacher_top,
        jnp.sum(teacher_total * jnp.exp(teacher_shift), axis=0, keepdims=True),
        jnp.sum(scale * (term + total * (shift - teacher_shift)), axis=0, keepdims=True),
    )


def grad_kernel(blocks, toks, place_ref, stats_ref, weight_ref, logits_ref, teacher_ref, own_ref, *refs):
    chunk_refs = refs[:-6]
    sums_ref, send_ref, diverge_ref, grad_ref, head_buf, sems = refs[-6:]
    side = place_ref[0]
    row = place_ref[1]
    step = 1 - 2 * side
    rest = toks - LANES
    groups = LANES // rest if rest else 1
    rows = 64 // groups
    depth = own_ref.shape[0] // HALVES
    sources = [own_ref.at[part * depth : (part + 1) * depth] for part in range(HALVES)] + list(chunk_refs)
    copies = [
        pltpu.make_async_copy(source, head_buf.at[index], sems.at[index]) for index, source in enumerate(sources)
    ]
    for copy in copies:
        copy.start()

    peak, total, teacher_peak, teacher_total, term = join(*[stats_ref[:, i, :toks] for i in range(5)])
    mean = term / total
    diverge_ref[...] = mean - jnp.log(total) + jnp.log(teacher_total)
    scale = loss_scale * weight_ref[:, :toks] / total
    offset = teacher_peak - mean
    table = jnp.concatenate([peak, scale, offset, jnp.zeros((LANES - 3, toks), jnp.float32)], axis=0)
    table = jnp.concatenate([table, jnp.zeros((LANES, 2 * LANES - toks), jnp.float32)], axis=1)
    columns = jnp.transpose(table)[:toks]
    shifted = logits_ref[:toks] - columns[:, 0:1]
    slope = shifted - teacher_ref[:toks].astype(jnp.float32) + columns[:, 2:3]
    grad = columns[:, 1:2] * jnp.exp(shifted) * slope
    grad_ref[...] = jnp.transpose(grad).astype(jnp.bfloat16)
    group = lax.broadcasted_iota(jnp.int32, (rows, LANES), 1) // max(rest, 1)

    def one(product, distance, part):
        owner = lax.rem(row - distance * step + blocks, blocks)
        first = lax.rem(owner, blocks // 2) * (HALVES * depth // 64) + part * (depth // 64)
        place = lax.rem(lax.div(owner, blocks // 2) + side, 2)
        for i in range(depth // 64):
            sums_ref[place, first + i, :64] = product[64 * i : 64 * i + 64, :LANES]
        if not rest:
            return
        wide = jnp.concatenate([product[:, LANES:], jnp.zeros((depth, LANES - rest), jnp.float32)], axis=1)
        for i in range(depth // 64):
            lower = wide[64 * i : 64 * i + rows]
            for near in range(1, groups):
                start = 64 * i + near * rows
                lower = jnp.where(group == near, pltpu.roll(wide[start : start + rows], near * rest, 1), lower)
            sums_ref[place, first + i, 64:] = lower

    for base in range(0, len(sources), WAITED):
        for index in range(base, base + WAITED):
            copies[index].wait()
        for index in range(base, base + WAITED):
            product = jnp.dot(head_buf[index], grad_ref[...], preferred_element_type=jnp.float32)
            one(product, index // HALVES, index % HALVES)
    send_ref[...] = sums_ref[1].astype(send_ref.dtype)


def grad_products(place, stats, weight, logits, teacher, own, chunks, blocks, count, toks):
    cols = logits.shape[1]
    width = own.shape[0] * blocks
    vmem = pl.BlockSpec(memory_space=pltpu.VMEM)
    hbm = pl.BlockSpec(memory_space=pltpu.HBM)
    shape = (count, toks // 2, LANES)
    large = [pltpu.with_memory_space_constraint(value, pltpu.HBM) for value in (own, *chunks)]
    return pl.pallas_call(
        functools.partial(grad_kernel, blocks, toks),
        out_shape=[
            jax.ShapeDtypeStruct((2,) + shape, jnp.float32),
            jax.ShapeDtypeStruct(shape, jnp.bfloat16),
            jax.ShapeDtypeStruct((1, toks), jnp.float32),
        ],
        in_specs=[pl.BlockSpec(memory_space=pltpu.SMEM)] + [vmem] * 4 + [hbm] * (1 + len(chunks)),
        out_specs=[vmem] * 3,
        scratch_shapes=[
            pltpu.VMEM((cols, toks), jnp.bfloat16),
            pltpu.VMEM((len(chunks) + HALVES, own.shape[0] // HALVES, cols), jnp.bfloat16),
            pltpu.SemaphoreType.DMA((len(chunks) + HALVES,)),
        ],
        compiler_params=pltpu.CompilerParams(vmem_limit_bytes=24 * 1024 * 1024),
        cost_estimate=pl.CostEstimate(
            flops=2 * toks * cols * width, bytes_accessed=2 * cols * width, transcendentals=toks * cols
        ),
    )(place, stats, weight, logits, teacher, *large)


def body(hidden, head, teacher_logits, lengths, slot_rollout, token_mask):
    tok_rows = hidden.shape[0]
    count = lax.axis_size("vocab")
    blocks = lax.axis_size("row")
    slot_count = tok_rows // WIN
    row_place = lax.axis_index("row")
    side_place = lax.axis_index("side")
    own_slots = lax.dynamic_slice_in_dim(slot_rollout, row_place * slot_count, slot_count)
    chosen = own_slots[:, None] == jnp.arange(lengths.shape[0], dtype=jnp.int32)[None, :]
    slot_length = jnp.sum(jnp.where(chosen, lengths[None, :], 0), axis=1)
    length_tok = jnp.repeat(slot_length, WIN)
    token = jnp.arange(tok_rows, dtype=jnp.int32)
    inside = (token_mask > 0) & (token % WIN < length_tok)
    weight = jnp.where(inside, 1.0 / length_tok.astype(jnp.float32), 0.0)

    earlier = token[None, :] < token[:, None]
    rank = jnp.sum((earlier & inside[None, :]).astype(jnp.int32), axis=1)
    spot = jnp.where(inside, rank, jnp.sum(inside.astype(jnp.int32)) + token - rank)
    pick = spot[None, :] == token[:, None]
    pick_low = pick.astype(jnp.bfloat16)
    hidden = jnp.dot(pick_low, hidden, preferred_element_type=jnp.float32).astype(jnp.bfloat16)
    teacher_logits = jnp.dot(pick_low, teacher_logits, preferred_element_type=jnp.float32).astype(jnp.bfloat16)
    weight = jnp.sum(jnp.where(pick, weight[None, :], 0.0), axis=1)
    most = jnp.full((8, LANES), jnp.sum(inside.astype(jnp.float32)))
    for apart in (1 << bit for bit in range((blocks - 1).bit_length())):
        most = jnp.maximum(most, lax.ppermute(most, "row", [(i, i ^ apart) for i in range(blocks)]))
    fits = most[0, 0] <= FEW

    full = head.shape[0]
    depth = full // HALVES
    ring = [(i, (i + 1) % blocks) for i in range(blocks)]
    ring += [(blocks + i, blocks + (i - 1) % blocks) for i in range(blocks)]
    step = 1 - 2 * side_place
    held = [head[part * depth : (part + 1) * depth] for part in range(HALVES)]
    logits = jnp.dot(
        lax.dynamic_slice_in_dim(hidden, row_place * full, full, axis=1), head, preferred_element_type=jnp.float32
    )
    chunks = []
    for distance in range(1, blocks):
        held = [lax.ppermute(part, ("side", "row"), ring) for part in held]
        owner = (row_place - distance * step + blocks) % blocks
        for part in range(HALVES):
            piece = lax.dynamic_slice_in_dim(hidden, owner * full + part * depth, depth, axis=1)
            logits = logits + jnp.dot(piece, held[part], preferred_element_type=jnp.float32)
        chunks += held

    teacher = teacher_logits.astype(jnp.float32)
    teacher_peak = jnp.max(teacher, axis=1)
    teacher_gap = teacher - teacher_peak[:, None]
    teacher_total = jnp.sum(jnp.exp(teacher_gap), axis=1)
    peak = jnp.max(logits, axis=1)
    shifted = logits - peak[:, None]
    powers = jnp.exp(shifted)
    total = jnp.sum(powers, axis=1)
    term = jnp.sum(powers * (shifted - teacher_gap), axis=1)
    blank = jnp.zeros_like(peak)
    own = jnp.stack([peak, total, teacher_peak, teacher_total, term, blank, blank, blank])
    other = swap_side(own)
    pair = jnp.concatenate([*join(*[jnp.stack([own[i], other[i]]) for i in range(5)]), own[5:]])
    stats = lax.all_to_all(jnp.broadcast_to(pair, (count,) + pair.shape), "vocab", 0, 0)

    place = jnp.stack([side_place, row_place]).astype(jnp.int32)

    def finish(toks, place, stats, weight, pick, logits, teacher_logits, head, *chunks):
        sums, send, diverge = grad_products(
            place, stats, weight[None], logits, teacher_logits, head, chunks, blocks, count, toks
        )
        packed = (sums[0] + swap_side(send).astype(jnp.float32)).astype(jnp.bfloat16)
        pieces = lax.all_to_all(packed, "vocab", 0, 0)
        summed = jnp.sum(pieces.astype(jnp.float32), axis=0).astype(jnp.bfloat16)
        rest = toks - LANES
        block = summed[:64]
        if rest:
            lower = jnp.concatenate([summed[64:, i : i + rest] for i in range(0, LANES, rest)], axis=0)
            block = jnp.concatenate([block, lower], axis=1)
        some = pick[:toks]
        block = jnp.dot(block, some.astype(jnp.bfloat16), preferred_element_type=jnp.float32).astype(jnp.bfloat16)
        loss = jnp.sum(jnp.where(some, (weight[:toks] * diverge[0])[:, None], 0.0), axis=0)
        return jnp.sum(loss.reshape(slot_count, WIN), axis=1), block.T

    stats, weight, pick = lax.optimization_barrier((stats, weight, pick))
    return lax.cond(
        fits,
        functools.partial(finish, FEW),
        functools.partial(finish, tok_rows),
        place, stats, weight, pick, logits, teacher_logits, head, *chunks,
    )


def solution(mesh):
    in_specs = (
        P("row", None),
        P("row", ("side", "vocab")),
        P("row", ("side", "vocab")),
        P(),
        P(),
        P("row"),
    )
    out_specs = (P("row"), P("row", ("side", "vocab")))
    return jax.shard_map(body, mesh=mesh, in_specs=in_specs, out_specs=out_specs, check_vma=False)
```

```python
import functools

import jax
import jax.numpy as jnp
from jax import lax
from jax.experimental import pallas as pl
from jax.experimental.pallas import tpu as pltpu
from jax.sharding import PartitionSpec as P

WIN = 16
HALVES = 2
WAITED = 4
FEW = 128
LANES = 128


loss_scale = 256.0


def swap_side(value):
    return lax.ppermute(value, "side", [(0, 1), (1, 0)])


def join(peak, total, teacher_peak, teacher_total, term):
    top = jnp.max(peak, axis=0, keepdims=True)
    teacher_top = jnp.max(teacher_peak, axis=0, keepdims=True)
    shift = peak - top
    teacher_shift = teacher_peak - teacher_top
    scale = jnp.exp(shift)
    return (
        top,
        jnp.sum(total * scale, axis=0, keepdims=True),
        teacher_top,
        jnp.sum(teacher_total * jnp.exp(teacher_shift), axis=0, keepdims=True),
        jnp.sum(scale * (term + total * (shift - teacher_shift)), axis=0, keepdims=True),
    )


def grad_kernel(blocks, toks, place_ref, stats_ref, weight_ref, logits_ref, teacher_ref, own_ref, *refs):
    chunk_refs = refs[:-6]
    sums_ref, send_ref, diverge_ref, grad_ref, head_buf, sems = refs[-6:]
    side = place_ref[0]
    row = place_ref[1]
    step = 1 - 2 * side
    rest = toks - LANES
    groups = LANES // rest if rest else 1
    rows = 64 // groups
    depth = own_ref.shape[0] // HALVES
    sources = [own_ref.at[part * depth : (part + 1) * depth] for part in range(HALVES)] + list(chunk_refs)
    copies = [
        pltpu.make_async_copy(source, head_buf.at[index], sems.at[index]) for index, source in enumerate(sources)
    ]
    for copy in copies:
        copy.start()

    peak, total, teacher_peak, teacher_total, term = join(*[stats_ref[:, i, :toks] for i in range(5)])
    mean = term / total
    diverge_ref[...] = mean - jnp.log(total) + jnp.log(teacher_total)
    scale = loss_scale * weight_ref[:, :toks] / total
    offset = teacher_peak - mean
    table = jnp.concatenate([peak, scale, offset, jnp.zeros((LANES - 3, toks), jnp.float32)], axis=0)
    table = jnp.concatenate([table, jnp.zeros((LANES, 2 * LANES - toks), jnp.float32)], axis=1)
    columns = jnp.transpose(table)[:toks]
    shifted = logits_ref[:toks] - columns[:, 0:1]
    slope = shifted - teacher_ref[:toks].astype(jnp.float32) + columns[:, 2:3]
    grad = columns[:, 1:2] * jnp.exp(shifted) * slope
    grad_ref[...] = jnp.transpose(grad).astype(jnp.bfloat16)
    group = lax.broadcasted_iota(jnp.int32, (rows, LANES), 1) // max(rest, 1)

    def one(product, distance, part):
        owner = lax.rem(row - distance * step + blocks, blocks)
        first = lax.rem(owner, blocks // 2) * (HALVES * depth // 64) + part * (depth // 64)
        place = lax.rem(lax.div(owner, blocks // 2) + side, 2)
        for i in range(depth // 64):
            sums_ref[place, first + i, :64] = product[64 * i : 64 * i + 64, :LANES]
        if not rest:
            return
        wide = jnp.concatenate([product[:, LANES:], jnp.zeros((depth, LANES - rest), jnp.float32)], axis=1)
        for i in range(depth // 64):
            lower = wide[64 * i : 64 * i + rows]
            for near in range(1, groups):
                start = 64 * i + near * rows
                lower = jnp.where(group == near, pltpu.roll(wide[start : start + rows], near * rest, 1), lower)
            sums_ref[place, first + i, 64:] = lower

    for base in range(0, len(sources), WAITED):
        for index in range(base, base + WAITED):
            copies[index].wait()
        for index in range(base, base + WAITED):
            product = jnp.dot(head_buf[index], grad_ref[...], preferred_element_type=jnp.float32)
            one(product, index // HALVES, index % HALVES)
    send_ref[...] = sums_ref[1].astype(send_ref.dtype)


def grad_products(place, stats, weight, logits, teacher, own, chunks, blocks, count, toks):
    cols = logits.shape[1]
    width = own.shape[0] * blocks
    vmem = pl.BlockSpec(memory_space=pltpu.VMEM)
    hbm = pl.BlockSpec(memory_space=pltpu.HBM)
    shape = (count, toks // 2, LANES)
    large = [pltpu.with_memory_space_constraint(value, pltpu.HBM) for value in (own, *chunks)]
    return pl.pallas_call(
        functools.partial(grad_kernel, blocks, toks),
        out_shape=[
            jax.ShapeDtypeStruct((2,) + shape, jnp.float32),
            jax.ShapeDtypeStruct(shape, jnp.bfloat16),
            jax.ShapeDtypeStruct((1, toks), jnp.float32),
        ],
        in_specs=[pl.BlockSpec(memory_space=pltpu.SMEM)] + [vmem] * 4 + [hbm] * (1 + len(chunks)),
        out_specs=[vmem] * 3,
        scratch_shapes=[
            pltpu.VMEM((cols, toks), jnp.bfloat16),
            pltpu.VMEM((len(chunks) + HALVES, own.shape[0] // HALVES, cols), jnp.bfloat16),
            pltpu.SemaphoreType.DMA((len(chunks) + HALVES,)),
        ],
        compiler_params=pltpu.CompilerParams(vmem_limit_bytes=24 * 1024 * 1024),
        cost_estimate=pl.CostEstimate(
            flops=2 * toks * cols * width, bytes_accessed=2 * cols * width, transcendentals=toks * cols
        ),
    )(place, stats, weight, logits, teacher, *large)


def body(hidden, head, teacher_logits, lengths, slot_rollout, token_mask):
    tok_rows = hidden.shape[0]
    count = lax.axis_size("vocab")
    blocks = lax.axis_size("row")
    slot_count = tok_rows // WIN
    row_place = lax.axis_index("row")
    side_place = lax.axis_index("side")
    own_slots = lax.dynamic_slice_in_dim(slot_rollout, row_place * slot_count, slot_count)
    chosen = own_slots[:, None] == jnp.arange(lengths.shape[0], dtype=jnp.int32)[None, :]
    slot_length = jnp.sum(jnp.where(chosen, lengths[None, :], 0), axis=1)
    length_tok = jnp.repeat(slot_length, WIN)
    token = jnp.arange(tok_rows, dtype=jnp.int32)
    inside = (token_mask > 0) & (token % WIN < length_tok)
    weight = jnp.where(inside, 1.0 / length_tok.astype(jnp.float32), 0.0)

    earlier = token[None, :] < token[:, None]
    rank = jnp.sum((earlier & inside[None, :]).astype(jnp.int32), axis=1)
    spot = jnp.where(inside, rank, jnp.sum(inside.astype(jnp.int32)) + token - rank)
    pick = spot[None, :] == token[:, None]
    pick_low = pick.astype(jnp.bfloat16)
    hidden = jnp.dot(pick_low, hidden, preferred_element_type=jnp.float32).astype(jnp.bfloat16)
    teacher_logits = jnp.dot(pick_low, teacher_logits, preferred_element_type=jnp.float32).astype(jnp.bfloat16)
    weight = jnp.sum(jnp.where(pick, weight[None, :], 0.0), axis=1)
    most = jnp.full((8, LANES), jnp.sum(inside.astype(jnp.float32)))

    full = head.shape[0]
    depth = full // HALVES
    ring = [(i, (i + 1) % blocks) for i in range(blocks)]
    ring += [(blocks + i, blocks + (i - 1) % blocks) for i in range(blocks)]
    step = 1 - 2 * side_place
    held = [head[part * depth : (part + 1) * depth] for part in range(HALVES)]
    logits = jnp.dot(
        lax.dynamic_slice_in_dim(hidden, row_place * full, full, axis=1), head, preferred_element_type=jnp.float32
    )
    chunks = []
    for distance in range(1, blocks):
        held = [lax.ppermute(part, ("side", "row"), ring) for part in held]
        apart = 1 << (distance // 2 - 1) if distance % 2 == 0 else blocks
        if apart < blocks:
            most = jnp.maximum(most, lax.ppermute(most, "row", [(i, i ^ apart) for i in range(blocks)]))
            held[0], most = lax.optimization_barrier((held[0], most))
        owner = (row_place - distance * step + blocks) % blocks
        for part in range(HALVES):
            piece = lax.dynamic_slice_in_dim(hidden, owner * full + part * depth, depth, axis=1)
            logits = logits + jnp.dot(piece, held[part], preferred_element_type=jnp.float32)
        chunks += held

    teacher = teacher_logits.astype(jnp.float32)
    teacher_peak = jnp.max(teacher, axis=1)
    teacher_gap = teacher - teacher_peak[:, None]
    teacher_total = jnp.sum(jnp.exp(teacher_gap), axis=1)
    peak = jnp.max(logits, axis=1)
    shifted = logits - peak[:, None]
    powers = jnp.exp(shifted)
    total = jnp.sum(powers, axis=1)
    term = jnp.sum(powers * (shifted - teacher_gap), axis=1)
    blank = jnp.zeros_like(peak)
    own = jnp.stack([peak, total, teacher_peak, teacher_total, term, blank, blank, blank])
    other = swap_side(own)
    pair = jnp.concatenate([*join(*[jnp.stack([own[i], other[i]]) for i in range(5)]), own[5:]])
    stats = lax.all_to_all(jnp.broadcast_to(pair, (count,) + pair.shape), "vocab", 0, 0)

    place = jnp.stack([side_place, row_place]).astype(jnp.int32)

    def finish(toks, place, stats, weight, pick, logits, teacher_logits, head, *chunks):
        sums, send, diverge = grad_products(
            place, stats, weight[None], logits, teacher_logits, head, chunks, blocks, count, toks
        )
        packed = (sums[0] + swap_side(send).astype(jnp.float32)).astype(jnp.bfloat16)
        pieces = lax.all_to_all(packed, "vocab", 0, 0)
        summed = jnp.sum(pieces.astype(jnp.float32), axis=0).astype(jnp.bfloat16)
        rest = toks - LANES
        block = summed[:64]
        if rest:
            lower = jnp.concatenate([summed[64:, i : i + rest] for i in range(0, LANES, rest)], axis=0)
            block = jnp.concatenate([block, lower], axis=1)
        some = pick[:toks]
        block = jnp.dot(block, some.astype(jnp.bfloat16), preferred_element_type=jnp.float32).astype(jnp.bfloat16)
        loss = jnp.sum(jnp.where(some, (weight[:toks] * diverge[0])[:, None], 0.0), axis=0)
        return jnp.sum(loss.reshape(slot_count, WIN), axis=1), block.T

    fits = most[0, 0] <= FEW
    stats, weight, pick = lax.optimization_barrier((stats, weight, pick))
    return lax.cond(
        fits,
        functools.partial(finish, FEW),
        functools.partial(finish, tok_rows),
        place, stats, weight, pick, logits, teacher_logits, head, *chunks,
    )


def solution(mesh):
    in_specs = (
        P("row", None),
        P("row", ("side", "vocab")),
        P("row", ("side", "vocab")),
        P(),
        P(),
        P("row"),
    )
    out_specs = (P("row"), P("row", ("side", "vocab")))
    return jax.shard_map(body, mesh=mesh, in_specs=in_specs, out_specs=out_specs, check_vma=False)
```

```python
import functools

import jax
import jax.numpy as jnp
from jax import lax
from jax.experimental import pallas as pl
from jax.experimental.pallas import tpu as pltpu
from jax.sharding import PartitionSpec as P

WIN = 16
HALVES = 2
WAITED = 4
FEW = 128
LANES = 128


loss_scale = 256.0


def swap_side(value):
    return lax.ppermute(value, "side", [(0, 1), (1, 0)])


def join(peak, total, teacher_peak, teacher_total, term):
    top = jnp.max(peak, axis=0, keepdims=True)
    teacher_top = jnp.max(teacher_peak, axis=0, keepdims=True)
    shift = peak - top
    teacher_shift = teacher_peak - teacher_top
    scale = jnp.exp(shift)
    return (
        top,
        jnp.sum(total * scale, axis=0, keepdims=True),
        teacher_top,
        jnp.sum(teacher_total * jnp.exp(teacher_shift), axis=0, keepdims=True),
        jnp.sum(scale * (term + total * (shift - teacher_shift)), axis=0, keepdims=True),
    )


def grad_kernel(blocks, toks, place_ref, stats_ref, weight_ref, logits_ref, teacher_ref, own_ref, *refs):
    chunk_refs = refs[:-6]
    sums_ref, send_ref, diverge_ref, grad_ref, head_buf, sems = refs[-6:]
    side = place_ref[0]
    row = place_ref[1]
    step = 1 - 2 * side
    rest = toks - LANES
    groups = LANES // rest if rest else 1
    rows = 64 // groups
    depth = own_ref.shape[0] // HALVES
    sources = [own_ref.at[part * depth : (part + 1) * depth] for part in range(HALVES)] + list(chunk_refs)
    copies = [
        pltpu.make_async_copy(source, head_buf.at[index], sems.at[index]) for index, source in enumerate(sources)
    ]
    for copy in copies:
        copy.start()

    peak, total, teacher_peak, teacher_total, term = join(*[stats_ref[:, i, :toks] for i in range(5)])
    mean = term / total
    diverge_ref[...] = mean - jnp.log(total) + jnp.log(teacher_total)
    scale = loss_scale * weight_ref[:, :toks] / total
    offset = teacher_peak - mean
    table = jnp.concatenate([peak, scale, offset, jnp.zeros((LANES - 3, toks), jnp.float32)], axis=0)
    table = jnp.concatenate([table, jnp.zeros((LANES, 2 * LANES - toks), jnp.float32)], axis=1)
    columns = jnp.transpose(table)[:toks]
    shifted = logits_ref[:toks] - columns[:, 0:1]
    slope = shifted - teacher_ref[:toks].astype(jnp.float32) + columns[:, 2:3]
    grad = columns[:, 1:2] * jnp.exp(shifted) * slope
    grad_ref[...] = jnp.transpose(grad).astype(jnp.bfloat16)
    group = lax.broadcasted_iota(jnp.int32, (rows, LANES), 1) // max(rest, 1)

    def one(product, distance, part):
        owner = lax.rem(row - distance * step + blocks, blocks)
        first = lax.rem(owner, blocks // 2) * (HALVES * depth // 64) + part * (depth // 64)
        place = lax.rem(lax.div(owner, blocks // 2) + side, 2)
        for i in range(depth // 64):
            sums_ref[place, first + i, :64] = product[64 * i : 64 * i + 64, :LANES]
        if not rest:
            return
        wide = jnp.concatenate([product[:, LANES:], jnp.zeros((depth, LANES - rest), jnp.float32)], axis=1)
        for i in range(depth // 64):
            lower = wide[64 * i : 64 * i + rows]
            for near in range(1, groups):
                start = 64 * i + near * rows
                lower = jnp.where(group == near, pltpu.roll(wide[start : start + rows], near * rest, 1), lower)
            sums_ref[place, first + i, 64:] = lower

    for base in range(0, len(sources), WAITED):
        for index in range(base, base + WAITED):
            copies[index].wait()
        for index in range(base, base + WAITED):
            product = jnp.dot(head_buf[index], grad_ref[...], preferred_element_type=jnp.float32)
            one(product, index // HALVES, index % HALVES)
    send_ref[...] = sums_ref[1].astype(send_ref.dtype)


def grad_products(place, stats, weight, logits, teacher, own, chunks, blocks, count, toks):
    cols = logits.shape[1]
    width = own.shape[0] * blocks
    vmem = pl.BlockSpec(memory_space=pltpu.VMEM)
    hbm = pl.BlockSpec(memory_space=pltpu.HBM)
    shape = (count, toks // 2, LANES)
    large = [pltpu.with_memory_space_constraint(value, pltpu.HBM) for value in (own, *chunks)]
    return pl.pallas_call(
        functools.partial(grad_kernel, blocks, toks),
        out_shape=[
            jax.ShapeDtypeStruct((2,) + shape, jnp.float32),
            jax.ShapeDtypeStruct(shape, jnp.bfloat16),
            jax.ShapeDtypeStruct((1, toks), jnp.float32),
        ],
        in_specs=[pl.BlockSpec(memory_space=pltpu.SMEM)] + [vmem] * 4 + [hbm] * (1 + len(chunks)),
        out_specs=[vmem] * 3,
        scratch_shapes=[
            pltpu.VMEM((cols, toks), jnp.bfloat16),
            pltpu.VMEM((len(chunks) + HALVES, own.shape[0] // HALVES, cols), jnp.bfloat16),
            pltpu.SemaphoreType.DMA((len(chunks) + HALVES,)),
        ],
        compiler_params=pltpu.CompilerParams(vmem_limit_bytes=24 * 1024 * 1024),
        cost_estimate=pl.CostEstimate(
            flops=2 * toks * cols * width, bytes_accessed=2 * cols * width, transcendentals=toks * cols
        ),
    )(place, stats, weight, logits, teacher, *large)


def body(hidden, head, teacher_logits, lengths, slot_rollout, token_mask):
    tok_rows = hidden.shape[0]
    count = lax.axis_size("vocab")
    blocks = lax.axis_size("row")
    slot_count = tok_rows // WIN
    row_place = lax.axis_index("row")
    side_place = lax.axis_index("side")
    own_slots = lax.dynamic_slice_in_dim(slot_rollout, row_place * slot_count, slot_count)
    chosen = own_slots[:, None] == jnp.arange(lengths.shape[0], dtype=jnp.int32)[None, :]
    slot_length = jnp.sum(jnp.where(chosen, lengths[None, :], 0), axis=1)
    length_tok = jnp.repeat(slot_length, WIN)
    token = jnp.arange(tok_rows, dtype=jnp.int32)
    inside = (token_mask > 0) & (token % WIN < length_tok)
    weight = jnp.where(inside, 1.0 / length_tok.astype(jnp.float32), 0.0)

    earlier = token[None, :] < token[:, None]
    rank = jnp.sum((earlier & inside[None, :]).astype(jnp.int32), axis=1)
    spot = jnp.where(inside, rank, jnp.sum(inside.astype(jnp.int32)) + token - rank)
    pick = spot[None, :] == token[:, None]
    pick_low = pick.astype(jnp.bfloat16)
    hidden = jnp.dot(pick_low, hidden, preferred_element_type=jnp.float32).astype(jnp.bfloat16)
    teacher_logits = jnp.dot(pick_low, teacher_logits, preferred_element_type=jnp.float32).astype(jnp.bfloat16)
    weight = jnp.sum(jnp.where(pick, weight[None, :], 0.0), axis=1)
    fits = jnp.sum(inside.astype(jnp.int32)) <= FEW

    full = head.shape[0]
    depth = full // HALVES
    ring = [(i, (i + 1) % blocks) for i in range(blocks)]
    ring += [(blocks + i, blocks + (i - 1) % blocks) for i in range(blocks)]
    step = 1 - 2 * side_place
    held = [head[part * depth : (part + 1) * depth] for part in range(HALVES)]
    logits = jnp.dot(
        lax.dynamic_slice_in_dim(hidden, row_place * full, full, axis=1), head, preferred_element_type=jnp.float32
    )
    chunks = []
    for distance in range(1, blocks):
        held = [lax.ppermute(part, ("side", "row"), ring) for part in held]
        if distance % 2 == 0:
            held[0], weight = lax.optimization_barrier((held[0], weight))
        owner = (row_place - distance * step + blocks) % blocks
        for part in range(HALVES):
            piece = lax.dynamic_slice_in_dim(hidden, owner * full + part * depth, depth, axis=1)
            logits = logits + jnp.dot(piece, held[part], preferred_element_type=jnp.float32)
        chunks += held

    teacher = teacher_logits.astype(jnp.float32)
    teacher_peak = jnp.max(teacher, axis=1)
    teacher_gap = teacher - teacher_peak[:, None]
    teacher_total = jnp.sum(jnp.exp(teacher_gap), axis=1)
    peak = jnp.max(logits, axis=1)
    shifted = logits - peak[:, None]
    powers = jnp.exp(shifted)
    total = jnp.sum(powers, axis=1)
    term = jnp.sum(powers * (shifted - teacher_gap), axis=1)
    blank = jnp.zeros_like(peak)
    own = jnp.stack([peak, total, teacher_peak, teacher_total, term, blank, blank, blank])
    other = swap_side(own)
    pair = jnp.concatenate([*join(*[jnp.stack([own[i], other[i]]) for i in range(5)]), own[5:]])
    stats = lax.all_to_all(jnp.broadcast_to(pair, (count,) + pair.shape), "vocab", 0, 0)

    place = jnp.stack([side_place, row_place]).astype(jnp.int32)

    def finish(toks, place, stats, weight, pick, logits, teacher_logits, head, *chunks):
        sums, send, diverge = grad_products(
            place, stats, weight[None], logits, teacher_logits, head, chunks, blocks, count, toks
        )
        packed = (sums[0] + swap_side(send).astype(jnp.float32)).astype(jnp.bfloat16)
        pieces = lax.all_to_all(packed, "vocab", 0, 0)
        summed = jnp.sum(pieces.astype(jnp.float32), axis=0).astype(jnp.bfloat16)
        rest = toks - LANES
        block = summed[:64]
        if rest:
            lower = jnp.concatenate([summed[64:, i : i + rest] for i in range(0, LANES, rest)], axis=0)
            block = jnp.concatenate([block, lower], axis=1)
        some = pick[:toks]
        block = jnp.dot(block, some.astype(jnp.bfloat16), preferred_element_type=jnp.float32).astype(jnp.bfloat16)
        loss = jnp.sum(jnp.where(some, (weight[:toks] * diverge[0])[:, None], 0.0), axis=0)
        return jnp.sum(loss.reshape(slot_count, WIN), axis=1), block.T

    stats, weight, pick = lax.optimization_barrier((stats, weight, pick))
    return lax.cond(
        fits,
        functools.partial(finish, FEW),
        functools.partial(finish, tok_rows),
        place, stats, weight, pick, logits, teacher_logits, head, *chunks,
    )


def solution(mesh):
    in_specs = (
        P("row", None),
        P("row", ("side", "vocab")),
        P("row", ("side", "vocab")),
        P(),
        P(),
        P("row"),
    )
    out_specs = (P("row"), P("row", ("side", "vocab")))
    return jax.shard_map(body, mesh=mesh, in_specs=in_specs, out_specs=out_specs, check_vma=False)
```

```python
import functools

import jax
import jax.numpy as jnp
from jax import lax
from jax.experimental import pallas as pl
from jax.experimental.pallas import tpu as pltpu
from jax.sharding import PartitionSpec as P

WIN = 16
HALVES = 2
WAITED = 4
FEW = 128
LANES = 128


loss_scale = 256.0


def swap_side(value):
    return lax.ppermute(value, "side", [(0, 1), (1, 0)])


def join(peak, total, teacher_peak, teacher_total, term):
    top = jnp.max(peak, axis=0, keepdims=True)
    teacher_top = jnp.max(teacher_peak, axis=0, keepdims=True)
    shift = peak - top
    teacher_shift = teacher_peak - teacher_top
    scale = jnp.exp(shift)
    return (
        top,
        jnp.sum(total * scale, axis=0, keepdims=True),
        teacher_top,
        jnp.sum(teacher_total * jnp.exp(teacher_shift), axis=0, keepdims=True),
        jnp.sum(scale * (term + total * (shift - teacher_shift)), axis=0, keepdims=True),
    )


def grad_kernel(blocks, toks, place_ref, stats_ref, weight_ref, logits_ref, teacher_ref, own_ref, *refs):
    chunk_refs = refs[:-6]
    sums_ref, send_ref, diverge_ref, grad_ref, head_buf, sems = refs[-6:]
    side = place_ref[0]
    row = place_ref[1]
    step = 1 - 2 * side
    rest = toks - LANES
    groups = LANES // rest if rest else 1
    rows = 64 // groups
    depth = own_ref.shape[0] // HALVES
    sources = [own_ref.at[part * depth : (part + 1) * depth] for part in range(HALVES)] + list(chunk_refs)
    copies = [
        pltpu.make_async_copy(source, head_buf.at[index], sems.at[index]) for index, source in enumerate(sources)
    ]
    for copy in copies:
        copy.start()

    peak, total, teacher_peak, teacher_total, term = join(*[stats_ref[:, i, :toks] for i in range(5)])
    mean = term / total
    diverge_ref[...] = mean - jnp.log(total) + jnp.log(teacher_total)
    scale = loss_scale * weight_ref[:, :toks] / total
    offset = teacher_peak - mean
    table = jnp.concatenate([peak, scale, offset, jnp.zeros((LANES - 3, toks), jnp.float32)], axis=0)
    table = jnp.concatenate([table, jnp.zeros((LANES, 2 * LANES - toks), jnp.float32)], axis=1)
    columns = jnp.transpose(table)[:toks]
    shifted = logits_ref[:toks] - columns[:, 0:1]
    slope = shifted - teacher_ref[:toks].astype(jnp.float32) + columns[:, 2:3]
    grad = columns[:, 1:2] * jnp.exp(shifted) * slope
    grad_ref[...] = jnp.transpose(grad).astype(jnp.bfloat16)
    group = lax.broadcasted_iota(jnp.int32, (rows, LANES), 1) // max(rest, 1)

    def one(product, distance, part):
        owner = lax.rem(row - distance * step + blocks, blocks)
        first = lax.rem(owner, blocks // 2) * (HALVES * depth // 64) + part * (depth // 64)
        place = lax.rem(lax.div(owner, blocks // 2) + side, 2)
        for i in range(depth // 64):
            sums_ref[place, first + i, :64] = product[64 * i : 64 * i + 64, :LANES]
        if not rest:
            return
        wide = jnp.concatenate([product[:, LANES:], jnp.zeros((depth, LANES - rest), jnp.float32)], axis=1)
        for i in range(depth // 64):
            lower = wide[64 * i : 64 * i + rows]
            for near in range(1, groups):
                start = 64 * i + near * rows
                lower = jnp.where(group == near, pltpu.roll(wide[start : start + rows], near * rest, 1), lower)
            sums_ref[place, first + i, 64:] = lower

    for base in range(0, len(sources), WAITED):
        for index in range(base, base + WAITED):
            copies[index].wait()
        for index in range(base, base + WAITED):
            product = jnp.dot(head_buf[index], grad_ref[...], preferred_element_type=jnp.float32)
            one(product, index // HALVES, index % HALVES)
    send_ref[...] = sums_ref[1].astype(send_ref.dtype)


def grad_products(place, stats, weight, logits, teacher, own, chunks, blocks, count, toks):
    cols = logits.shape[1]
    width = own.shape[0] * blocks
    vmem = pl.BlockSpec(memory_space=pltpu.VMEM)
    hbm = pl.BlockSpec(memory_space=pltpu.HBM)
    shape = (count, toks // 2, LANES)
    large = [pltpu.with_memory_space_constraint(value, pltpu.HBM) for value in (own, *chunks)]
    return pl.pallas_call(
        functools.partial(grad_kernel, blocks, toks),
        out_shape=[
            jax.ShapeDtypeStruct((2,) + shape, jnp.float32),
            jax.ShapeDtypeStruct(shape, jnp.bfloat16),
            jax.ShapeDtypeStruct((1, toks), jnp.float32),
        ],
        in_specs=[pl.BlockSpec(memory_space=pltpu.SMEM)] + [vmem] * 4 + [hbm] * (1 + len(chunks)),
        out_specs=[vmem] * 3,
        scratch_shapes=[
            pltpu.VMEM((cols, toks), jnp.bfloat16),
            pltpu.VMEM((len(chunks) + HALVES, own.shape[0] // HALVES, cols), jnp.bfloat16),
            pltpu.SemaphoreType.DMA((len(chunks) + HALVES,)),
        ],
        compiler_params=pltpu.CompilerParams(vmem_limit_bytes=24 * 1024 * 1024),
        cost_estimate=pl.CostEstimate(
            flops=2 * toks * cols * width, bytes_accessed=2 * cols * width, transcendentals=toks * cols
        ),
    )(place, stats, weight, logits, teacher, *large)


def body(hidden, head, teacher_logits, lengths, slot_rollout, token_mask):
    tok_rows = hidden.shape[0]
    count = lax.axis_size("vocab")
    blocks = lax.axis_size("row")
    slot_count = tok_rows // WIN
    row_place = lax.axis_index("row")
    side_place = lax.axis_index("side")
    own_slots = lax.dynamic_slice_in_dim(slot_rollout, row_place * slot_count, slot_count)
    chosen = own_slots[:, None] == jnp.arange(lengths.shape[0], dtype=jnp.int32)[None, :]
    slot_length = jnp.sum(jnp.where(chosen, lengths[None, :], 0), axis=1)
    length_tok = jnp.repeat(slot_length, WIN)
    token = jnp.arange(tok_rows, dtype=jnp.int32)
    inside = (token_mask > 0) & (token % WIN < length_tok)
    weight = jnp.where(inside, 1.0 / length_tok.astype(jnp.float32), 0.0)

    earlier = token[None, :] < token[:, None]
    rank = jnp.sum((earlier & inside[None, :]).astype(jnp.int32), axis=1)
    spot = jnp.where(inside, rank, jnp.sum(inside.astype(jnp.int32)) + token - rank)
    pick = spot[None, :] == token[:, None]
    pick_low = pick.astype(jnp.bfloat16)
    hidden = jnp.dot(pick_low, hidden, preferred_element_type=jnp.float32).astype(jnp.bfloat16)
    teacher_logits = jnp.dot(pick_low, teacher_logits, preferred_element_type=jnp.float32).astype(jnp.bfloat16)
    weight = jnp.sum(jnp.where(pick, weight[None, :], 0.0), axis=1)
    fits = jnp.sum(inside.astype(jnp.int32)) <= FEW

    full = head.shape[0]
    depth = full // HALVES
    ring = [(i, (i + 1) % blocks) for i in range(blocks)]
    ring += [(blocks + i, blocks + (i - 1) % blocks) for i in range(blocks)]
    step = 1 - 2 * side_place
    held = [head[part * depth : (part + 1) * depth] for part in range(HALVES)]
    logits = jnp.dot(
        lax.dynamic_slice_in_dim(hidden, row_place * full, full, axis=1), head, preferred_element_type=jnp.float32
    )
    chunks = []
    for distance in range(1, blocks):
        held = [lax.ppermute(part, ("side", "row"), ring) for part in held]
        if distance % 2 == 0:
            held[0], weight = lax.optimization_barrier((held[0], weight))
        owner = (row_place - distance * step + blocks) % blocks
        for part in range(HALVES):
            piece = lax.dynamic_slice_in_dim(hidden, owner * full + part * depth, depth, axis=1)
            logits = logits + jnp.dot(piece, held[part], preferred_element_type=jnp.float32)
        chunks += held

    teacher = teacher_logits.astype(jnp.float32)
    teacher_peak = jnp.max(teacher, axis=1)
    teacher_gap = teacher - teacher_peak[:, None]
    teacher_total = jnp.sum(jnp.exp(teacher_gap), axis=1)
    peak = jnp.max(logits, axis=1)
    shifted = logits - peak[:, None]
    powers = jnp.exp(shifted)
    total = jnp.sum(powers, axis=1)
    term = jnp.sum(powers * (shifted - teacher_gap), axis=1)
    blank = jnp.zeros_like(peak)
    own = jnp.stack([peak, total, teacher_peak, teacher_total, term, blank, blank, blank])
    place = jnp.stack([side_place, row_place]).astype(jnp.int32)

    def finish(toks, place, own, weight, pick, logits, teacher_logits, head, *chunks):
        own = own[:, :toks]
        other = swap_side(own)
        pair = jnp.concatenate([*join(*[jnp.stack([own[i], other[i]]) for i in range(5)]), own[5:]])
        stats = lax.all_to_all(jnp.broadcast_to(pair, (count,) + pair.shape), "vocab", 0, 0)
        sums, send, diverge = grad_products(
            place, stats, weight[None], logits, teacher_logits, head, chunks, blocks, count, toks
        )
        packed = (sums[0] + swap_side(send).astype(jnp.float32)).astype(jnp.bfloat16)
        pieces = lax.all_to_all(packed, "vocab", 0, 0)
        summed = jnp.sum(pieces.astype(jnp.float32), axis=0).astype(jnp.bfloat16)
        rest = toks - LANES
        block = summed[:64]
        if rest:
            lower = jnp.concatenate([summed[64:, i : i + rest] for i in range(0, LANES, rest)], axis=0)
            block = jnp.concatenate([block, lower], axis=1)
        some = pick[:toks]
        block = jnp.dot(block, some.astype(jnp.bfloat16), preferred_element_type=jnp.float32).astype(jnp.bfloat16)
        loss = jnp.sum(jnp.where(some, (weight[:toks] * diverge[0])[:, None], 0.0), axis=0)
        return jnp.sum(loss.reshape(slot_count, WIN), axis=1), block.T

    own, weight, pick = lax.optimization_barrier((own, weight, pick))
    return lax.cond(
        fits,
        functools.partial(finish, FEW),
        functools.partial(finish, tok_rows),
        place, own, weight, pick, logits, teacher_logits, head, *chunks,
    )


def solution(mesh):
    in_specs = (
        P("row", None),
        P("row", ("side", "vocab")),
        P("row", ("side", "vocab")),
        P(),
        P(),
        P("row"),
    )
    out_specs = (P("row"), P("row", ("side", "vocab")))
    return jax.shard_map(body, mesh=mesh, in_specs=in_specs, out_specs=out_specs, check_vma=False)
```
